32 devices in a mesh: dp: 4 (over y, x), expert: 8 (over z, core).
Axes of the slice: x: 2, y: 2, z: 4, core: 2. Of those that a mesh axis runs over, the one named last changes fastest.
Arguments:
- target_in: bfloat16 [20480, 1408], P(('dp', 'expert')), may hold values from -6 to 6
- ln_gain: float32 [1408], replicated, may hold values from 0.1 to 1.9
- up_target: bfloat16 [1408, 3072], P('dp'), may hold values from -0.15625 to 0.15625
- down_target: bfloat16 [3072, 1408], P('dp'), may hold values from -0.109375 to 0.109375
- pred_rows: bfloat16 [3072, 1024], P('expert'), may hold values from -6 to 6
- expert_ids: int32 [3072, 2], P('expert'), may hold values from 0 to 31, all different within a row; in each aligned block of 384 rows (0 to 383, 384 to 767, ...) at most 32 rows name the same one
- combine_weights: float32 [3072, 2], P('expert'), may hold values from 0.25 to 1
- gate_experts: bfloat16 [32, 2816, 1024], P(('dp', 'expert')), may hold values from -0.1875 to 0.1875
- up_experts: bfloat16 [32, 2816, 1024], P(('dp', 'expert')), may hold values from -0.1875 to 0.1875
- down_experts: bfloat16 [32, 2816, 1024], P(('dp', 'expert')), may hold values from -0.21875 to 0.21875
Outputs:
- target_out: bfloat16 [20480, 1408], P(('dp', 'expert'))
- predicted: bfloat16 [3072, 1024], P('expert', 'dp')
The draws below stay inside these ranges and needn't reach their ends.
Inputs may be any that keep to these rules, and one draw needn't show every extreme that they name: `expert_ids`: each row names 2 different experts. Within each aligned block of 384 rows (the rows of one device) no expert is named by more than 32 rows, a bound that some block reaches.
All inputs are finite; a program needn't handle non-finite values.
Results may differ from the reference program's by a relative error of at most 0.004.
Values may be sent and summed in bfloat16 or wider, within the bound.
No kernel may reach another device: no remote copies, remote signals or barrier semaphores. Data moves between devices by JAX's collectives and lax.ppermute only.
A program may use at most 128 MiB of HBM per device.

```python
import math
import jax
import jax.numpy as jnp
import numpy as np
from jax import lax

D_T = 1408
FF_T = 3072
TT_DEV = 640
D_M = 1024
FF_M = 2816
TOP = 2
MR_DEV = 384
CAP = 32
EXPERTS = 32
SLICES = 1
T_ROWS = 20480
ROWS_M = 3072
N_EXPERT = 8


def spiked(entries, rng, source, target, parts, factor):
    owner, partner = [(jnp.arange(entries.shape[dim]) // (entries.shape[dim] // parts)).reshape([-1 if axis == dim else 1 for axis in range(entries.ndim)]) for dim in (source, target)]
    chosen = jax.random.permutation(rng, parts)[partner]
    strong = (owner == chosen) | (owner == (partner + parts // 2) % parts)
    return jnp.where(strong, factor * entries, entries)


def steps_of(own_key, shape, cuts, least, top_value):
    factor_of = 1.0
    for axis_at, shards_of in cuts:
        steps = jax.random.uniform(jax.random.fold_in(jax.random.fold_in(own_key, 6), axis_at), (shards_of,), jnp.float32, least / len(cuts), top_value / len(cuts))
        factor_of = factor_of * jnp.repeat(jnp.exp(steps), shape[axis_at] // shards_of).reshape((-1,) + (1,) * (len(shape) - 1 - axis_at))
    return factor_of


def shared_out(rng, own, number, rows, number_of, top, reach, slope):
    order = jax.random.permutation(rng, number_of)
    crowded, common = portions_of(number_of, rows * top, reach, slope, True), portions_of(number_of, rows * top, reach, slope, False)
    places = jnp.arange(number_of)

    def named(sizes, offset_by):
        used = int((sizes > 0).sum())
        fixed = max(1, used // 4)
        shifted = fixed + (places - fixed + offset_by * (used - fixed)) % max(1, number_of - fixed)
        return jnp.zeros((number_of,), jnp.int32).at[order[jnp.where(places < fixed, places, shifted)]].set(jnp.asarray(sizes, jnp.int32))

    sizes = jnp.where(number % 4 == 0, named(crowded, number // 4), named(common, number - number // 4 - 1))
    mixed = jax.random.permutation(jax.random.fold_in(own, 3), number_of)
    giver, sink = mixed[0:number_of // 2 * 2:2], mixed[1:number_of // 2 * 2:2]
    room = jnp.minimum(sizes[giver] - 1, reach - sizes[sink]) // 2
    room = jnp.where((giver == order[0]) | (sink == order[0]) | (sizes[sink] == 0), 0, jnp.maximum(room, 0))
    shifted = jax.random.randint(jax.random.fold_in(own, 4), (number_of // 2,), 0, 1 << 20) % (room + 1)
    sizes = sizes.at[giver].add(-shifted).at[sink].add(shifted)
    items = jnp.searchsorted(jnp.cumsum(sizes), jnp.arange(rows * top), side="right").astype(jnp.int32)
    grid = items.reshape(top, rows).T
    grid = grid[jax.random.permutation(jax.random.fold_in(own, 1), rows)]
    offset_by = jax.random.randint(jax.random.fold_in(own, 2), (rows, 1), 0, top)
    return jnp.take_along_axis(grid, (jnp.arange(top)[None, :] + offset_by) % top, axis=1)


def portions_of(count, total, most, slope, full):
    portions = [(1 << 20) // math.isqrt(rank ** slope) + 1 for rank in range(1, count + 1)]
    largest = most if full else min(most, max(-(-total // count), total * portions[0] // sum(portions)))
    least = 1 if total - largest >= count - 1 else 0
    holding, rest = [largest] + [least] * (count - 1), total - largest - least * (count - 1)
    while rest > 0:
        free = [i for i in range(1, count) if holding[i] < largest] or [i for i in range(1, count) if holding[i] < most]
        whole, remaining = sum([portions[i] for i in free]), rest
        for i in free:
            extra = min(most - holding[i], max(1, remaining * portions[i] // whole), rest)
            holding[i] = holding[i] + extra
            rest = rest - extra
    return np.array(holding)


def bell_draw(stream_key, extent, deviation, reach, pieces=(), kind=jnp.bfloat16):
    drawn = deviation * jax.random.normal(stream_key, extent, jnp.float32)
    if pieces:
        drawn = drawn * steps_of(stream_key, extent, pieces, -0.22, 0.18)
    return jnp.clip(drawn, -reach, reach).astype(kind)


def gaussian_with(stream_key, dims, scale, limit, shards, heavy, kind=jnp.bfloat16):
    result = scale * jax.random.normal(stream_key, dims, jnp.float32)
    if shards:
        result = result * steps_of(stream_key, dims, shards, -0.22, 0.18)
    return jnp.clip(spiked(result, jax.random.fold_in(stream_key, 3), *heavy), -limit, limit).astype(kind)


def setup_inputs(seed: int = 0) -> dict:
    arg_keys = jax.random.split(jax.random.key(seed), 11)
    target_in = bell_draw(arg_keys[0], (T_ROWS, D_T), 1.0, 6.0, ((0, 32),))
    ln_gain = jnp.clip(1.0 + 0.18 * jax.random.normal(arg_keys[1], (D_T,), jnp.float32), 0.1, 1.9)
    up_target = bell_draw(arg_keys[2], (D_T, FF_T), D_T ** -0.5, 0.15625, ((0, 4),))
    down_target = bell_draw(arg_keys[3], (FF_T, D_T), FF_T ** -0.5, 0.109375, ((0, 4),))
    pred_rows = bell_draw(arg_keys[4], (ROWS_M, D_M), 1.0, 6.0, ((0, 8),))
    expert_ids_keys = jax.random.split(jax.random.fold_in(arg_keys[5], 1), ROWS_M // MR_DEV)
    expert_ids_turns = jax.random.permutation(jax.random.fold_in(arg_keys[5], 3), ROWS_M // MR_DEV)
    expert_ids = jax.vmap(lambda own, number: shared_out(jax.random.fold_in(arg_keys[5], 2), own, number, MR_DEV, EXPERTS, TOP, CAP, 2))(expert_ids_keys, expert_ids_turns).reshape((ROWS_M, TOP))
    combine_weights = jnp.clip(0.25 + 0.75 * jax.random.uniform(arg_keys[6], (ROWS_M, TOP), jnp.float32) ** steps_of(arg_keys[6], (ROWS_M, TOP), ((0, 8),), -0.2, 0.2), 0.25, 1.0)
    gate_experts = bell_draw(arg_keys[7], (SLICES * EXPERTS, FF_M // SLICES, D_M), D_M ** -0.5, 0.1875, ((0, 32),))
    up_experts = bell_draw(arg_keys[8], (SLICES * EXPERTS, FF_M // SLICES, D_M), D_M ** -0.5, 0.1875, ((0, 32),))
    down_experts = gaussian_with(arg_keys[9], (SLICES * EXPERTS, FF_M // SLICES, D_M), FF_M ** -0.5, 0.21875, ((0, 32),), (0, 2, 32, 2.75))
    return dict(target_in=target_in, ln_gain=ln_gain, up_target=up_target, down_target=down_target, pred_rows=pred_rows, expert_ids=expert_ids, combine_weights=combine_weights, gate_experts=gate_experts, up_experts=up_experts, down_experts=down_experts)


def target_block(block_rows, ln_gain, up_target, down_target):
    values = block_rows.astype(jnp.float32)
    average = lax.optimization_barrier(jnp.mean(values, axis=-1, keepdims=True))
    centered = values - average
    variance = lax.optimization_barrier(jnp.mean(centered * centered, axis=-1, keepdims=True))
    normed = (centered * lax.rsqrt(variance + 1e-06) * ln_gain).astype(jnp.bfloat16)
    pre_act = jnp.dot(normed, up_target, preferred_element_type=jnp.float32)
    hidden = jax.nn.gelu(pre_act, approximate=True).astype(jnp.bfloat16)
    projected = jnp.dot(hidden, down_target, preferred_element_type=jnp.float32)
    return (values + projected).astype(jnp.bfloat16)

def reference(target_in, ln_gain, up_target, down_target, pred_rows, expert_ids, combine_weights, gate_experts, up_experts, down_experts):
    blocks = target_in.reshape(T_ROWS // TT_DEV, TT_DEV, D_T)
    target_out = lax.map(lambda block_rows: target_block(block_rows, ln_gain, up_target, down_target), blocks)
    target_out = target_out.reshape(T_ROWS, D_T)
    gate_view = gate_experts.reshape(SLICES, EXPERTS, FF_M // SLICES, D_M)
    up_view = up_experts.reshape(SLICES, EXPERTS, FF_M // SLICES, D_M)
    down_view = down_experts.reshape(SLICES, EXPERTS, FF_M // SLICES, D_M)
    contract = (((1,), (1,)), ((), ()))

    def expert_block(operands):
        slot_rows, which = operands
        gate_w = lax.dynamic_index_in_dim(gate_view, which, 1, keepdims=False).reshape(FF_M, D_M)
        up_w = lax.dynamic_index_in_dim(up_view, which, 1, keepdims=False).reshape(FF_M, D_M)
        down_w = lax.dynamic_index_in_dim(down_view, which, 1, keepdims=False).reshape(FF_M, D_M)
        gate_vals = lax.dot_general(slot_rows, gate_w, contract, preferred_element_type=jnp.float32)
        up_vals = lax.dot_general(slot_rows, up_w, contract, preferred_element_type=jnp.float32)
        inner_act = (jax.nn.silu(gate_vals) * up_vals).astype(jnp.bfloat16)
        return jnp.dot(inner_act, down_w, preferred_element_type=jnp.float32)
    flat_ids = expert_ids.reshape(N_EXPERT, MR_DEV * TOP)
    onehot = (flat_ids[:, :, None] == jnp.arange(EXPERTS, dtype=jnp.int32)[None, None, :]).astype(jnp.int32)
    running = jnp.cumsum(onehot, axis=1) - onehot
    slot_index = lax.optimization_barrier(jnp.sum(running * onehot, axis=2)).astype(jnp.int32)
    source_dev = jnp.arange(N_EXPERT, dtype=jnp.int32)[:, None]
    position = ((flat_ids * N_EXPERT + source_dev) * CAP + slot_index).reshape(-1).astype(jnp.int32)
    row_index = jnp.arange(ROWS_M * TOP, dtype=jnp.int32) // TOP
    buffers = jnp.zeros((EXPERTS * N_EXPERT * CAP, D_M), jnp.bfloat16).at[position].set(pred_rows[row_index])
    buffers = buffers.reshape(EXPERTS, N_EXPERT * CAP, D_M)
    expert_out = lax.map(expert_block, (buffers, jnp.arange(EXPERTS, dtype=jnp.int32)))
    picked = expert_out.reshape(EXPERTS * N_EXPERT * CAP, D_M)[position].reshape(ROWS_M, TOP, D_M)
    mixed_out = lax.optimization_barrier(jnp.sum(picked * combine_weights[:, :, None], axis=1))
    predicted = (pred_rows.astype(jnp.float32) + mixed_out).astype(jnp.bfloat16)
    return (target_out, predicted)
```

```python
import jax
import jax.numpy as jnp
from jax import lax
from jax.sharding import PartitionSpec as P

EXP_DEV = 4
TOP = 2
CAP = 32
BF = jnp.bfloat16
F32 = jnp.float32


def xor_perm(size, bits):
    return [(i, i ^ bits) for i in range(size)]


def norm_rows(rows, gain):
    values = rows.astype(F32)
    average = jnp.mean(values, axis=-1, keepdims=True)
    centered = values - average
    variance = jnp.mean(centered * centered, axis=-1, keepdims=True)
    return (centered * lax.rsqrt(variance + 1e-06) * gain).astype(BF)


def dot(a, b):
    return jnp.dot(a, b, preferred_element_type=F32)


def feed_forward(normed, up, down):
    hidden = jax.nn.gelu(dot(normed, up), approximate=True).astype(BF)
    return dot(hidden, down)


def target_gathered(target_in, ln_gain, up_target, down_target):
    normed = norm_rows(target_in, ln_gain)
    projected = feed_forward(
        normed,
        lax.all_gather(up_target, "dp", axis=0, tiled=True),
        lax.all_gather(down_target, "dp", axis=0, tiled=True),
    )
    return (target_in.astype(F32) + projected).astype(BF)


def target_square(target_in, ln_gain, up_target, down_target):
    depth, width = up_target.shape
    block = width // 4
    half = block // 2
    me = lax.axis_index("dp")
    core = lax.axis_index("expert") % 2
    n_exp = lax.axis_size("expert")
    px, py, pc = xor_perm(4, 1), xor_perm(4, 2), xor_perm(n_exp, 1)

    other_in = lax.ppermute(target_in, "expert", pc)

    def place(pieces, rows):
        out = jnp.zeros((4 * rows, pieces[0].shape[1]), BF)
        for i, piece in enumerate(pieces):
            out = lax.dynamic_update_slice(out, piece, ((me ^ i) * rows, 0))
        return out

    own_sum = other_sum = None
    weights = []
    for start, count in ((0, 256), (256, 128)):
        up_0 = jnp.concatenate(
            [
                lax.dynamic_slice(
                    up_target, (0, b * block + core * half + start), (depth, count)
                )
                for b in range(4)
            ],
            axis=1,
        )
        down_0 = lax.dynamic_slice(
            down_target, (core * half + start, 0), (count, down_target.shape[1])
        )
        up_x, up_y = lax.ppermute(up_0, "dp", px), lax.ppermute(up_0, "dp", py)
        down_x, down_y = lax.ppermute(down_0, "dp", px), lax.ppermute(down_0, "dp", py)
        up_d, down_d = lax.ppermute(up_y, "dp", px), lax.ppermute(down_x, "dp", py)
        weights.append((
            place([up_0, up_x, up_y, up_d], depth),
            place([down_0, down_x, down_y, down_d], count),
        ))
    other_n = norm_rows(other_in, ln_gain)
    own_n = norm_rows(target_in, ln_gain)
    other_sum = sum(feed_forward(other_n, *w) for w in weights)
    own_sum = sum(feed_forward(own_n, *w) for w in weights)
    received = lax.ppermute(other_sum.astype(BF), "expert", pc)
    return (target_in.astype(F32) + own_sum + received.astype(F32)).astype(BF)


def exchange(blocks, axis, size):
    me = lax.axis_index(axis)
    out = jnp.zeros_like(blocks)
    out = lax.dynamic_update_index_in_dim(
        out, lax.dynamic_index_in_dim(blocks, me, 0, keepdims=False), me, 0
    )
    for bits in range(1, size):
        sent = lax.dynamic_index_in_dim(blocks, me ^ bits, 0, keepdims=False)
        got = lax.ppermute(sent, axis, xor_perm(size, bits))
        out = lax.dynamic_update_index_in_dim(out, got, me ^ bits, 0)
    return out


def experts_part(
    pred_rows, expert_ids, combine_weights, gate_experts, up_experts, down_experts
):
    owners = lax.axis_size("expert")
    n_dp = lax.axis_size("dp")
    rows, width = pred_rows.shape
    n_all = EXP_DEV * owners
    group = lax.axis_index("dp") % EXP_DEV
    chosen = expert_ids.T
    each = jnp.arange(n_all, dtype=jnp.int32)[:, None]
    named_k = [chosen[k][None, :] == each for k in range(TOP)]
    named = named_k[0]
    for more in named_k[1:]:
        named = named | more
    before = jnp.arange(rows)[:, None] < jnp.arange(rows)[None, :]
    slot = dot(named.astype(BF), before.astype(BF)).astype(jnp.int32)
    slot = jnp.where(named, slot, -1)
    spread = slot[:, None, :] == jnp.arange(CAP, dtype=jnp.int32)[None, :, None]
    mine = lax.dynamic_slice_in_dim(slot, group * owners, owners, 0)
    pick = mine[:, None, :] == jnp.arange(CAP, dtype=jnp.int32)[None, :, None]
    pick = pick.reshape(owners * CAP, rows).astype(BF)
    outgoing = dot(pick, pred_rows).astype(BF)
    slot_rows = exchange(
        outgoing.reshape(owners, CAP, width), "expert", owners
    ).reshape(owners * CAP, width)
    contract = (((1,), (1,)), ((), ()))
    gate_vals = lax.dot_general(
        slot_rows, gate_experts[0], contract, preferred_element_type=F32
    )
    up_vals = lax.dot_general(
        slot_rows, up_experts[0], contract, preferred_element_type=F32
    )
    inner_act = (jax.nn.silu(gate_vals) * up_vals).astype(BF)
    partial_out = dot(inner_act, down_experts[0]).astype(BF)
    share = width // n_dp
    by_cols = partial_out.reshape(owners * CAP, n_dp, share).transpose(1, 0, 2)
    by_cols = exchange(by_cols, "dp", n_dp)
    by_rows = by_cols.reshape(n_dp, owners, CAP * share).transpose(1, 0, 2)
    back = exchange(by_rows, "expert", owners)
    back = back.reshape(owners, n_dp, CAP, share).transpose(1, 0, 2, 3)
    back = back.reshape(n_dp // EXP_DEV, n_all * CAP, share)
    if n_dp > EXP_DEV:
        back = jnp.sum(back.astype(F32), axis=0)
    else:
        back = back[0]
    mixed_out = 0.0
    weight = sum(
        jnp.where(named_k[k], combine_weights[:, k][None, :], 0.0) for k in range(TOP)
    )
    mix = jnp.where(spread, weight[:, None, :], 0.0).reshape(n_all * CAP, rows)
    over = (((0,), (0,)), ((), ()))
    high = mix.astype(BF)
    low = (mix - high.astype(F32)).astype(BF)
    if n_dp > EXP_DEV:
        mixed_out = lax.dot_general(
            mix, back, over, precision=lax.Precision.HIGHEST, preferred_element_type=F32
        )
    else:
        mixed_out = lax.dot_general(
            high, back, over, preferred_element_type=F32
        ) + lax.dot_general(low, back, over, preferred_element_type=F32)
    residual = lax.dynamic_slice_in_dim(
        pred_rows, lax.axis_index("dp") * share, share, 1
    ).astype(F32)
    return (residual + mixed_out).astype(BF)


def solution(mesh):
    square = mesh.shape["dp"] == 4 and mesh.shape["expert"] % 2 == 0
    target_part = target_square if square else target_gathered

    def on_device(
        target_in,
        ln_gain,
        up_target,
        down_target,
        pred_rows,
        expert_ids,
        combine_weights,
        gate_experts,
        up_experts,
        down_experts,
    ):
        predicted = experts_part(
            pred_rows,
            expert_ids,
            combine_weights,
            gate_experts,
            up_experts,
            down_experts,
        )
        target_out = target_part(target_in, ln_gain, up_target, down_target)
        return (target_out, predicted)

    in_specs = (
        P(("dp", "expert"), None),
        P(),
        P("dp", None),
        P("dp", None),
        P("expert", None),
        P("expert", None),
        P("expert", None),
        P(("dp", "expert"), None, None),
        P(("dp", "expert"), None, None),
        P(("dp", "expert"), None, None),
    )
    out_specs = (P(("dp", "expert"), None), P("expert", "dp"))
    return jax.shard_map(
        on_device, mesh=mesh, in_specs=in_specs, out_specs=out_specs, check_vma=False
    )
```

```python
import jax
import jax.numpy as jnp
from jax import lax
from jax.experimental import pallas as pl
from jax.experimental.pallas import tpu as pltpu
from jax.sharding import PartitionSpec as P

EXP_DEV = 4
TOP = 2
CAP = 32
BF = jnp.bfloat16
F32 = jnp.float32


def xor_perm(size, bits):
    return [(i, i ^ bits) for i in range(size)]


def norm_rows(rows, gain):
    values = rows.astype(F32)
    average = jnp.mean(values, axis=-1, keepdims=True)
    centered = values - average
    variance = jnp.mean(centered * centered, axis=-1, keepdims=True)
    return (centered * lax.rsqrt(variance + 1e-06) * gain).astype(BF)


def dot(a, b):
    return jnp.dot(a, b, preferred_element_type=F32)


def feed_forward(normed, up, down):
    hidden = jax.nn.gelu(dot(normed, up), approximate=True).astype(BF)
    return dot(hidden, down)


def target_gathered(target_in, ln_gain, up_target, down_target):
    normed = norm_rows(target_in, ln_gain)
    projected = feed_forward(
        normed,
        lax.all_gather(up_target, "dp", axis=0, tiled=True),
        lax.all_gather(down_target, "dp", axis=0, tiled=True),
    )
    return (target_in.astype(F32) + projected).astype(BF)


def after(value, *others):
    return lax.optimization_barrier((value, others))[0]


def gelu(v):
    return 0.5 * v * (1.0 + jnp.tanh(0.7978845608028654 * (v + 0.044715 * (v * v * v))))


def cut_up_kernel(at_ref, up_ref, top_ref, low_ref):
    rows = top_ref.shape[0]
    top_ref[...] = up_ref[:rows, :]
    low_ref[...] = up_ref[rows:, :]


def cut_up(at, up_target):
    depth, width = up_target.shape
    part = jax.ShapeDtypeStruct((depth // 2, width // 2), BF)
    block = width // 8
    out = pl.BlockSpec((depth // 2, block), lambda j, at: (0, j))
    return pl.pallas_call(
        cut_up_kernel,
        out_shape=(part, part),
        grid_spec=pltpu.PrefetchScalarGridSpec(
            num_scalar_prefetch=1,
            grid=(4,),
            in_specs=[
                pl.BlockSpec((depth, block), lambda j, at: (0, (at[0] ^ j) * 2 + at[1]))
            ],
            out_specs=(out, out),
        ),
        compiler_params=pltpu.CompilerParams(vmem_limit_bytes=8 * 2**20),
        cost_estimate=pl.CostEstimate(
            flops=0, bytes_accessed=2 * depth * width, transcendentals=0
        ),
        name="cut_up",
    )(at, up_target)


def up_kernel(at_ref, other_ref, own_ref, *refs):
    pieces, (out_ref, x_ref, w_ref, sem, x_sem) = refs[:8], refs[8:]
    step = pl.program_id(0)
    depth, width = pieces[0].shape
    block = width // 4
    me = at_ref[0]
    rows = own_ref.shape[0]
    tile = out_ref.shape[1]
    x_made = [
        pltpu.make_async_copy(ref, x_ref.at[pl.ds(i * rows, rows)], x_sem.at[i])
        for i, ref in enumerate((other_ref, own_ref))
    ]

    def copies(n):
        found = []
        for j in (2 * n, 2 * n + 1):
            for p, piece in enumerate(pieces):
                i, h = p // 2, p % 2
                row = pl.multiple_of(((me ^ i) * 2 + h) * depth, 16)
                found.append(
                    pltpu.make_async_copy(
                        piece.at[:, pl.ds((j ^ i) * block, block)],
                        w_ref.at[pl.ds(row, depth), pl.ds(j * block, block)],
                        sem.at[n, len(found)],
                    )
                )
        return found

    @pl.when(step == 0)
    def _():
        for c in copies(0) + x_made + copies(1):
            c.start()
        for c in copies(0) + x_made:
            c.wait()

    @pl.when(step == pl.num_programs(0) // 2)
    def _():
        for c in copies(1):
            c.wait()

    w = w_ref[:, pl.ds(pl.multiple_of(step * tile, tile), tile)]
    out_ref[...] = gelu(dot(x_ref[...], w)).astype(BF)


def up_call(at, other_n, own_n, pieces):
    rows, depth = own_n.shape
    width = pieces[0].shape[1]
    tile = 256
    hbm = pl.BlockSpec(memory_space=pltpu.HBM)
    return pl.pallas_call(
        up_kernel,
        out_shape=jax.ShapeDtypeStruct((2 * rows, width), BF),
        grid=(width // tile,),
        in_specs=[pl.BlockSpec(memory_space=pltpu.SMEM)] + [hbm] * 10,
        out_specs=pl.BlockSpec((2 * rows, tile), lambda n: (0, n)),
        scratch_shapes=[
            pltpu.VMEM((2 * rows, depth), BF),
            pltpu.VMEM((depth, width), BF),
            pltpu.SemaphoreType.DMA((2, 16)),
            pltpu.SemaphoreType.DMA((2,)),
        ],
        compiler_params=pltpu.CompilerParams(vmem_limit_bytes=20 * 2**20),
        cost_estimate=pl.CostEstimate(
            flops=8 * rows * depth * width, bytes_accessed=12 * 10**6, transcendentals=0
        ),
        name="up",
    )(at, other_n, own_n, *pieces)


def down_kernel(h_ref, *refs):
    pieces, (out_ref, w_ref, sem) = refs[:6], refs[6:]
    count = pieces[0].shape[0]

    @pl.when(pl.program_id(0) == 0)
    def _():
        made = [
            pltpu.make_async_copy(piece, w_ref.at[pl.ds(i * count, count)], sem.at[i])
            for i, piece in enumerate(pieces)
        ]
        for c in made:
            c.start()
        for c in made:
            c.wait()

    out_ref[...] = dot(h_ref[:, : 6 * count], w_ref[...])


def down_call(hidden, pieces):
    rows, width = hidden.shape
    count, wide = pieces[0].shape
    tile = 320
    return pl.pallas_call(
        down_kernel,
        out_shape=jax.ShapeDtypeStruct((rows, wide), F32),
        grid=(rows // tile,),
        in_specs=[pl.BlockSpec((tile, width), lambda m: (m, 0))]
        + [pl.BlockSpec(memory_space=pltpu.HBM)] * 6,
        out_specs=pl.BlockSpec((tile, wide), lambda m: (m, 0)),
        scratch_shapes=[
            pltpu.VMEM((6 * count, wide), BF),
            pltpu.SemaphoreType.DMA((6,)),
        ],
        compiler_params=pltpu.CompilerParams(vmem_limit_bytes=20 * 2**20),
        cost_estimate=pl.CostEstimate(
            flops=16 * rows * count * wide, bytes_accessed=15 * 10**6, transcendentals=0
        ),
        name="down",
    )(hidden, *pieces)


def last_kernel(h_ref, da, db, sum_ref, *refs):
    top = da.shape[0]
    out_ref = refs[-1]
    total = sum_ref[...] + dot(h_ref[:, :top], da[...]) + dot(h_ref[:, top:], db[...])
    if len(refs) == 2:
        total = total + refs[0][...].astype(F32)
    out_ref[...] = total.astype(out_ref.dtype)


def last_call(hidden, da, db, sums, first, rows_in, dtype):
    top, wide = da.shape
    count = hidden.shape[1] // 4
    rows, tile = hidden.shape[0] // 2, 320
    skip = first // tile
    whole = pl.BlockSpec((top, wide), lambda m: (0, 0))
    extra = [] if rows_in is None else [rows_in]
    return pl.pallas_call(
        last_kernel,
        out_shape=jax.ShapeDtypeStruct((rows, wide), dtype),
        grid=(rows // tile,),
        in_specs=[
            pl.BlockSpec((tile, count), lambda m: (m + skip, 3)),
            whole,
            whole,
            pl.BlockSpec((tile, wide), lambda m: (m + skip, 0)),
        ]
        + [pl.BlockSpec((tile, wide), lambda m: (m, 0)) for _ in extra],
        out_specs=pl.BlockSpec((tile, wide), lambda m: (m, 0)),
        compiler_params=pltpu.CompilerParams(vmem_limit_bytes=24 * 2**20),
        cost_estimate=pl.CostEstimate(
            flops=3 * rows * count * wide, bytes_accessed=6 * 10**6, transcendentals=0
        ),
        name="last",
    )(hidden, da, db, sums, *extra)


def program_square(
    target_in,
    ln_gain,
    up_target,
    down_target,
    pred_rows,
    expert_ids,
    combine_weights,
    gate_experts,
    up_experts,
    down_experts,
):
    depth, width = up_target.shape
    block = width // 4
    half = block // 2
    wide = down_target.shape[1]
    me = lax.axis_index("dp")
    core = lax.axis_index("expert") % 2
    px, py = xor_perm(4, 1), xor_perm(4, 2)
    pc = xor_perm(lax.axis_size("expert"), 1)

    at = jnp.stack([me, core]).astype(jnp.int32)

    def both(parts):
        return [lax.ppermute(parts[h], "dp", p) for p in (px, py) for h in range(2)]

    ups = cut_up(at, up_target)
    ux_t, ux_b, uy_t, uy_b = both(ups)
    dispatched = lax.all_to_all(
        dispatch_rows(pred_rows, expert_ids), "expert", 0, 0, tiled=True
    )
    other_in = lax.ppermute(target_in, "expert", pc)
    ud_t, ud_b = lax.ppermute(uy_t, "dp", px), lax.ppermute(ux_b, "dp", py)
    part = half // 2
    downs = [
        lax.dynamic_slice(down_target, (core * half + h * part, 0), (part, wide))
        for h in range(2)
    ]
    dx_t, dx_b, dy_t, dy_b = both([after(d, ux_b, uy_t) for d in downs])
    dd_t, dd_b = lax.ppermute(dy_t, "dp", px), lax.ppermute(dx_b, "dp", py)
    other_n, own_n = norm_rows(other_in, ln_gain), norm_rows(target_in, ln_gain)
    dispatched = after(dispatched, ux_b, uy_t, other_n, own_n)
    by_cols = expert_call(dispatched, gate_experts, up_experts, down_experts)
    back = lax.all_to_all(by_cols, ("dp", "expert"), 0, 0, tiled=True)
    hidden = up_call(
        at,
        after(other_n, by_cols),
        own_n,
        (*ups, ux_t, ux_b, uy_t, uy_b, ud_t, ud_b),
    )
    sums = down_call(hidden, (*downs, dx_t, dx_b, dy_t, dy_b))
    predicted = combine(pred_rows, expert_ids, combine_weights, back)
    sums = after(sums, predicted)
    rows = target_in.shape[0]
    other_sum = last_call(hidden, dd_t, dd_b, sums, 0, None, BF)
    received = lax.ppermute(other_sum, "expert", pc)
    own_sum = last_call(hidden, dd_t, dd_b, sums, rows, target_in, F32)
    return (own_sum + received.astype(F32)).astype(BF), predicted


def slots_of(expert_ids, rows, n_all):
    chosen = expert_ids.T
    each = jnp.arange(n_all, dtype=jnp.int32)[:, None]
    named_k = [chosen[k][None, :] == each for k in range(TOP)]
    named = named_k[0]
    for more in named_k[1:]:
        named = named | more
    before = jnp.arange(rows)[:, None] < jnp.arange(rows)[None, :]
    slot = dot(named.astype(BF), before.astype(BF)).astype(jnp.int32)
    return named_k, jnp.where(named, slot, -1)


def dispatch_rows(pred_rows, expert_ids):
    owners = lax.axis_size("expert")
    rows, width = pred_rows.shape
    group = lax.axis_index("dp") % EXP_DEV
    _, slot = slots_of(expert_ids - group * owners, rows, owners)
    pick = slot[:, None, :] == jnp.arange(CAP, dtype=jnp.int32)[None, :, None]
    pick = pick.reshape(owners * CAP, rows).astype(BF)
    return dot(pick, pred_rows).astype(BF).reshape(owners, CAP, width)


def expert_kernel(x_ref, g_ref, u_ref, d_ref, out_ref, total):
    step = pl.program_id(0)
    contract = (((1,), (1,)), ((), ()))
    x = x_ref[...]
    gate = lax.dot_general(x, g_ref[0], contract, preferred_element_type=F32)
    up = lax.dot_general(x, u_ref[0], contract, preferred_element_type=F32)
    act = (gate / (1.0 + jnp.exp(-gate)) * up).astype(BF)
    part = dot(act, d_ref[0])

    @pl.when(step == 0)
    def _():
        total[...] = part

    @pl.when(step > 0)
    def _():
        total[...] += part

    @pl.when(step == pl.num_programs(0) - 1)
    def _():
        if len(out_ref.shape) == 2:
            out_ref[...] = total[...].astype(BF)
        else:
            share = out_ref.shape[2]
            for d in range(out_ref.shape[0]):
                out_ref[d] = total[:, d * share : (d + 1) * share].astype(BF)


def expert_call(dispatched, gate_experts, up_experts, down_experts):
    owners, cap, width = dispatched.shape
    n_dp = lax.axis_size("dp")
    share = width // n_dp
    rows = owners * cap
    hidden = gate_experts.shape[1]
    tile = 704 if hidden % 704 == 0 else hidden
    whole = share % 128 == 0
    shape = (n_dp, rows, share) if whole else (rows, width)
    weights = pl.BlockSpec((1, tile, width), lambda i: (0, i, 0))
    out = pl.pallas_call(
        expert_kernel,
        out_shape=jax.ShapeDtypeStruct(shape, BF),
        grid=(hidden // tile,),
        in_specs=[pl.BlockSpec((rows, width), lambda i: (0, 0))] + [weights] * 3,
        out_specs=pl.BlockSpec(shape, lambda i: (0,) * len(shape)),
        scratch_shapes=[pltpu.VMEM((rows, width), F32)],
        compiler_params=pltpu.CompilerParams(vmem_limit_bytes=24 * 2**20),
        cost_estimate=pl.CostEstimate(
            flops=6 * rows * hidden * width,
            bytes_accessed=6 * hidden * width + 4 * rows * width,
            transcendentals=0,
        ),
        name="expert",
    )(
        dispatched.reshape(rows, width),
        *[
            pltpu.with_memory_space_constraint(w, pltpu.HBM)
            for w in (gate_experts, up_experts, down_experts)
        ],
    )
    if not whole:
        out = out.reshape(rows, n_dp, share).transpose(1, 0, 2)
    return out.reshape(n_dp * owners, cap, share)


def combine(pred_rows, expert_ids, combine_weights, back):
    owners = lax.axis_size("expert")
    n_dp = lax.axis_size("dp")
    rows, width = pred_rows.shape
    n_all = EXP_DEV * owners
    share = width // n_dp
    named_k, slot = slots_of(expert_ids, rows, n_all)
    spread = slot[:, None, :] == jnp.arange(CAP, dtype=jnp.int32)[None, :, None]
    weight = sum(
        jnp.where(named_k[k], combine_weights[:, k][None, :], 0.0) for k in range(TOP)
    )
    mix = jnp.where(spread, weight[:, None, :], 0.0).reshape(n_all * CAP, rows)
    over = (((0,), (0,)), ((), ()))
    high = mix.astype(BF)
    low = (mix - high.astype(F32)).astype(BF)
    mixed_out = 0.0
    back = back.reshape(n_dp // EXP_DEV, n_all * CAP, share)
    for q in range(n_dp // EXP_DEV):
        for part in (high, low):
            mixed_out = mixed_out + lax.dot_general(
                part, back[q], over, preferred_element_type=F32
            )
    residual = lax.dynamic_slice_in_dim(
        pred_rows, lax.axis_index("dp") * share, share, 1
    ).astype(F32)
    return (residual + mixed_out).astype(BF)


def program_any(
    target_in,
    ln_gain,
    up_target,
    down_target,
    pred_rows,
    expert_ids,
    combine_weights,
    gate_experts,
    up_experts,
    down_experts,
):
    dispatched = lax.all_to_all(
        dispatch_rows(pred_rows, expert_ids), "expert", 0, 0, tiled=True
    )
    by_cols = expert_call(dispatched, gate_experts, up_experts, down_experts)
    back = lax.all_to_all(by_cols, ("dp", "expert"), 0, 0, tiled=True)
    predicted = combine(pred_rows, expert_ids, combine_weights, back)
    target_out = target_gathered(target_in, ln_gain, up_target, down_target)
    return target_out, predicted


def solution(mesh):
    square = mesh.shape["dp"] == 4 and mesh.shape["expert"] % 2 == 0
    on_device = program_square if square else program_any

    in_specs = (
        P(("dp", "expert"), None),
        P(),
        P("dp", None),
        P("dp", None),
        P("expert", None),
        P("expert", None),
        P("expert", None),
        P(("dp", "expert"), None, None),
        P(("dp", "expert"), None, None),
        P(("dp", "expert"), None, None),
    )
    out_specs = (P(("dp", "expert"), None), P("expert", "dp"))
    return jax.shard_map(
        on_device, mesh=mesh, in_specs=in_specs, out_specs=out_specs, check_vma=False
    )
```

```python
import jax
import jax.numpy as jnp
from jax import lax
from jax.experimental import pallas as pl
from jax.experimental.pallas import tpu as pltpu
from jax.sharding import PartitionSpec as P

EXP_DEV = 4
TOP = 2
CAP = 32
BF = jnp.bfloat16
F32 = jnp.float32


def xor_perm(size, bits):
    return [(i, i ^ bits) for i in range(size)]


def norm_rows(rows, gain):
    values = rows.astype(F32)
    average = jnp.mean(values, axis=-1, keepdims=True)
    centered = values - average
    variance = jnp.mean(centered * centered, axis=-1, keepdims=True)
    return (centered * lax.rsqrt(variance + 1e-06) * gain).astype(BF)


def dot(a, b):
    return jnp.dot(a, b, preferred_element_type=F32)


def feed_forward(normed, up, down):
    hidden = jax.nn.gelu(dot(normed, up), approximate=True).astype(BF)
    return dot(hidden, down)


def target_gathered(target_in, ln_gain, up_target, down_target):
    normed = norm_rows(target_in, ln_gain)
    projected = feed_forward(
        normed,
        lax.all_gather(up_target, "dp", axis=0, tiled=True),
        lax.all_gather(down_target, "dp", axis=0, tiled=True),
    )
    return (target_in.astype(F32) + projected).astype(BF)


ANYWHERE = pl.BlockSpec(memory_space=pl.ANY)


def in_hbm(*arrays):
    return [pltpu.with_memory_space_constraint(a, pltpu.HBM) for a in arrays]


def halves_kernel(waited_ref, first_ref, second_ref, top_ref, low_ref):
    top_ref[...] = first_ref[...]
    low_ref[...] = second_ref[...]


def halves(waited, first, second):
    rows, width = first.shape
    part = jax.ShapeDtypeStruct((rows // 2, width), first.dtype)
    tile = width // 2 if width % 256 == 0 else width
    out = pl.BlockSpec((rows // 2, tile), lambda i: (0, i))
    return pl.pallas_call(
        halves_kernel,
        out_shape=(part, part),
        grid=(width // tile,),
        in_specs=[
            ANYWHERE,
            pl.BlockSpec((rows // 2, tile), lambda i: (0, i)),
            pl.BlockSpec((rows // 2, tile), lambda i: (1, i)),
        ],
        out_specs=(out, out),
        compiler_params=pltpu.CompilerParams(vmem_limit_bytes=8 * 2**20),
        cost_estimate=pl.CostEstimate(flops=1, bytes_accessed=1, transcendentals=0),
        name="halves",
    )(*in_hbm(waited), first, second)


def hold_kernel(*refs):
    pass


def hold(waited, *arrays):
    n = len(arrays)
    return pl.pallas_call(
        hold_kernel,
        out_shape=[jax.ShapeDtypeStruct(a.shape, a.dtype) for a in arrays],
        in_specs=[ANYWHERE] * (n + 1),
        out_specs=[ANYWHERE] * n,
        input_output_aliases={i + 1: i for i in range(n)},
        compiler_params=pltpu.CompilerParams(vmem_limit_bytes=2**20),
        cost_estimate=pl.CostEstimate(flops=1, bytes_accessed=1, transcendentals=0),
        name="hold",
    )(*in_hbm(waited), *arrays)


def gelu(v):
    return 0.5 * v * (1.0 + jnp.tanh(0.7978845608028654 * (v + 0.044715 * (v * v * v))))


def cut_down_kernel(at_ref, down_ref, *refs):
    for place, ref in enumerate(refs[-2:]):

        @pl.when(pl.program_id(0) == place)
        def _():
            ref[...] = down_ref[...]


def cut_down(at, down_target, waited):
    count, wide = down_target.shape
    part = jax.ShapeDtypeStruct((count // 4, wide), BF)
    out = pl.BlockSpec((count // 4, wide), lambda i, at: (0, 0))
    return pl.pallas_call(
        cut_down_kernel,
        out_shape=(part, part),
        grid_spec=pltpu.PrefetchScalarGridSpec(
            num_scalar_prefetch=1,
            grid=(2,),
            in_specs=[
                pl.BlockSpec((count // 4, wide), lambda i, at: (at[1] * 2 + i, 0)),
                ANYWHERE,
            ],
            out_specs=(out, out),
        ),
        compiler_params=pltpu.CompilerParams(vmem_limit_bytes=8 * 2**20),
        cost_estimate=pl.CostEstimate(flops=1, bytes_accessed=1, transcendentals=0),
        name="cut_down",
    )(at, *in_hbm(down_target, waited))


def norm_kernel(waited_ref, other_ref, own_ref, gain_ref, out_ref):
    for place, ref in enumerate((other_ref, own_ref)):

        @pl.when(pl.program_id(0) == place)
        def _():
            out_ref[...] = norm_rows(ref[...], gain_ref[...])


def norm_call(waited, other_in, target_in, ln_gain):
    rows, depth = target_in.shape
    tile = 320
    steps = rows // tile
    return pl.pallas_call(
        norm_kernel,
        out_shape=pltpu.HBM((2 * rows, depth), BF),
        grid=(2, steps),
        in_specs=[
            ANYWHERE,
            pl.BlockSpec((tile, depth), lambda i, m: ((1 - i) * m + i * (steps - 1), 0)),
            pl.BlockSpec((tile, depth), lambda i, m: (i * m, 0)),
            pl.BlockSpec((1, depth), lambda i, m: (0, 0)),
        ],
        out_specs=pl.BlockSpec((tile, depth), lambda i, m: (i * steps + m, 0)),
        compiler_params=pltpu.CompilerParams(vmem_limit_bytes=16 * 2**20),
        cost_estimate=pl.CostEstimate(flops=1, bytes_accessed=1, transcendentals=0),
        name="norm",
    )(*in_hbm(waited), other_in, target_in, ln_gain[None])


def cut_kernel(at_ref, whole_ref, *refs):
    refs[-1][...] = whole_ref[...]


def cut_up(at, up_target):
    depth, width = up_target.shape
    block = width // 8
    return pl.pallas_call(
        cut_kernel,
        out_shape=jax.ShapeDtypeStruct((depth, width // 2), BF),
        grid_spec=pltpu.PrefetchScalarGridSpec(
            num_scalar_prefetch=1,
            grid=(4,),
            in_specs=[
                pl.BlockSpec((depth, block), lambda j, at: (0, (at[0] ^ j) * 2 + at[1]))
            ],
            out_specs=pl.BlockSpec((depth, block), lambda j, at: (0, j)),
        ),
        compiler_params=pltpu.CompilerParams(vmem_limit_bytes=8 * 2**20),
        cost_estimate=pl.CostEstimate(flops=1, bytes_accessed=1, transcendentals=0),
        name="cut_up",
    )(at, *in_hbm(up_target))


def up_kernel(waited_ref, x_ref, *refs):
    pieces, (out_ref, w_ref, sem) = refs[:5], refs[5:]
    m, n = pl.program_id(0), pl.program_id(1)
    depth, width = pieces[0].shape
    block = width // 4
    me = lax.axis_index("dp")

    def copies(n):
        found = []
        for j in (2 * n, 2 * n + 1):
            for p, piece in enumerate(pieces):
                i, rows = min(p, 3), piece.shape[0]
                row = pl.multiple_of((me ^ i) * depth + (p // 4) * rows, 16)
                found.append(
                    pltpu.make_async_copy(
                        piece.at[:, pl.ds((j ^ i) * block, block)],
                        w_ref.at[n, pl.ds(row, rows), pl.ds((j % 2) * block, block)],
                        sem.at[n, len(found)],
                    )
                )
        return found

    @pl.when((m == 0) & (n == 0))
    def _():
        for c in copies(0) + copies(1):
            c.start()
        for c in copies(0):
            c.wait()

    @pl.when((m == 0) & (n == 1))
    def _():
        for c in copies(1):
            c.wait()

    out_ref[...] = gelu(dot(x_ref[...], w_ref[n])).astype(BF)


def up_call(waited, normed, pieces):
    rows, depth = normed.shape
    width = pieces[0].shape[1]
    tile = 640
    return pl.pallas_call(
        up_kernel,
        out_shape=pltpu.HBM((rows, width), BF),
        grid=(rows // tile, 2),
        in_specs=[ANYWHERE, pl.BlockSpec((tile, depth), lambda m, n: (m, 0))]
        + [ANYWHERE] * 5,
        out_specs=pl.BlockSpec((tile, width // 2), lambda m, n: (m, n)),
        scratch_shapes=[
            pltpu.VMEM((2, depth, width // 2), BF),
            pltpu.SemaphoreType.DMA((2, 10)),
        ],
        compiler_params=pltpu.CompilerParams(vmem_limit_bytes=60 * 2**20),
        cost_estimate=pl.CostEstimate(flops=1, bytes_accessed=1, transcendentals=0),
        name="up",
    )(*in_hbm(waited, normed), *pieces)


def down_kernel(waited_ref, h_ref, *refs):
    pieces, (out_ref, w_ref, sem) = refs[:6], refs[6:]
    count = pieces[0].shape[0]

    @pl.when(pl.program_id(0) == 0)
    def _():
        made = [
            pltpu.make_async_copy(piece, w_ref.at[pl.ds(i * count, count)], sem.at[i])
            for i, piece in enumerate(pieces)
        ]
        for c in made:
            c.start()
        for c in made:
            c.wait()

    out_ref[...] = dot(h_ref[:, : 6 * count], w_ref[...])


def down_call(waited, hidden, pieces):
    rows, width = hidden.shape
    count, wide = pieces[0].shape
    tile = 320
    return pl.pallas_call(
        down_kernel,
        out_shape=jax.ShapeDtypeStruct((rows, wide), F32),
        grid=(rows // tile,),
        in_specs=[ANYWHERE, pl.BlockSpec((tile, width), lambda m: (m, 0))]
        + [ANYWHERE] * 6,
        out_specs=pl.BlockSpec((tile, wide), lambda m: (m, 0)),
        scratch_shapes=[
            pltpu.VMEM((6 * count, wide), BF),
            pltpu.SemaphoreType.DMA((6,)),
        ],
        compiler_params=pltpu.CompilerParams(vmem_limit_bytes=20 * 2**20),
        cost_estimate=pl.CostEstimate(flops=1, bytes_accessed=1, transcendentals=0),
        name="down",
    )(*in_hbm(waited, hidden), *pieces)


def last_kernel(waited_ref, h_ref, da, db, sum_ref, *refs):
    top = da.shape[0]
    *more, out_ref = refs
    total = sum_ref[...] + dot(h_ref[:, :top], da[...]) + dot(h_ref[:, top:], db[...])
    for ref in more:
        total = total + ref[...].astype(F32)
    out_ref[...] = total.astype(out_ref.dtype)


def last_call(waited, hidden, da, db, sums, first, rows_in, dtype):
    top, wide = da.shape
    count = hidden.shape[1] // 4
    rows, tile = hidden.shape[0] // 2, 320
    skip = first // tile
    whole = pl.BlockSpec((top, wide), lambda m: (0, 0))
    extra = [] if rows_in is None else [rows_in]
    return pl.pallas_call(
        last_kernel,
        out_shape=jax.ShapeDtypeStruct((rows, wide), dtype),
        grid=(rows // tile,),
        in_specs=[
            ANYWHERE,
            pl.BlockSpec((tile, count), lambda m: (m + skip, 3)),
            whole,
            whole,
            pl.BlockSpec((tile, wide), lambda m: (m + skip, 0)),
        ]
        + [pl.BlockSpec((tile, wide), lambda m: (m, 0)) for _ in extra],
        out_specs=pl.BlockSpec((tile, wide), lambda m: (m, 0)),
        compiler_params=pltpu.CompilerParams(vmem_limit_bytes=24 * 2**20),
        cost_estimate=pl.CostEstimate(flops=1, bytes_accessed=1, transcendentals=0),
        name="last",
    )(waited, *in_hbm(hidden), da, db, sums, *extra)


def program_square(
    target_in,
    ln_gain,
    up_target,
    down_target,
    pred_rows,
    expert_ids,
    combine_weights,
    gate_experts,
    up_experts,
    down_experts,
):
    depth, width = up_target.shape
    block = width // 4
    half = block // 2
    wide = down_target.shape[1]
    me = lax.axis_index("dp")
    core = lax.axis_index("expert") % 2
    px, py = xor_perm(4, 1), xor_perm(4, 2)
    pc = xor_perm(lax.axis_size("expert"), 1)

    at = jnp.stack([me, core]).astype(jnp.int32)

    def both(piece):
        return lax.ppermute(piece, "dp", px), lax.ppermute(piece, "dp", py)

    up_0 = cut_up(at, up_target)
    up_x, up_y = both(up_0)
    ids_t, weights_t = expert_ids.T, combine_weights.T
    other_in = lax.ppermute(target_in, "expert", pc)
    outgoing = send_call(up_0, pred_rows, ids_t)
    dispatched = lax.all_to_all(outgoing, "expert", 0, 0, tiled=True)
    normed = norm_call(outgoing, other_in, target_in, ln_gain)
    upper, lower = halves(normed, up_y, up_x)
    ud_t, ud_b = lax.ppermute(upper, "dp", px), lax.ppermute(lower, "dp", py)
    d_t, d_b = hold(upper, *cut_down(at, down_target, normed))
    dx_t, dy_t = both(d_t)
    dx_b, dy_b = both(d_b)
    by_cols = expert_call(
        dispatched, gate_experts, up_experts, down_experts, *in_hbm(upper)
    )
    back = lax.all_to_all(by_cols, ("dp", "expert"), 0, 0, tiled=True)
    hidden = up_call(by_cols, normed, (up_0, up_x, up_y, ud_t, ud_b))
    dx_b, dy_t = hold(hidden, dx_b, dy_t)
    dd_t, dd_b = lax.ppermute(dy_t, "dp", px), lax.ppermute(dx_b, "dp", py)
    predicted = mix_call(at, hidden, pred_rows, ids_t, weights_t, back)
    sums = down_call(predicted, hidden, (d_t, d_b, dx_t, dx_b, dy_t, dy_b))
    rows = target_in.shape[0]
    other_sum = last_call(*in_hbm(predicted), hidden, dd_t, dd_b, sums, 0, None, BF)
    received = lax.ppermute(other_sum, "expert", pc)
    own_sum = last_call(other_sum, hidden, dd_t, dd_b, sums, rows, target_in, F32)
    return (own_sum + received.astype(F32)).astype(BF), predicted


def slots_of(expert_ids, rows, n_all):
    chosen = expert_ids.T
    each = jnp.arange(n_all, dtype=jnp.int32)[:, None]
    named_k = [chosen[k][None, :] == each for k in range(TOP)]
    named = named_k[0]
    for more in named_k[1:]:
        named = named | more
    before = jnp.arange(rows)[:, None] < jnp.arange(rows)[None, :]
    slot = dot(named.astype(BF), before.astype(BF)).astype(jnp.int32)
    return named_k, jnp.where(named, slot, -1)


def dispatch_rows(pred_rows, expert_ids):
    owners = lax.axis_size("expert")
    rows, width = pred_rows.shape
    group = lax.axis_index("dp") % EXP_DEV
    _, slot = slots_of(expert_ids - group * owners, rows, owners)
    pick = slot[:, None, :] == jnp.arange(CAP, dtype=jnp.int32)[None, :, None]
    pick = pick.reshape(owners * CAP, rows).astype(BF)
    return dot(pick, pred_rows).astype(BF).reshape(owners, CAP, width)


def expert_kernel(x_ref, g_ref, u_ref, d_ref, *refs):
    out_ref, total = refs[-2:]
    step = pl.program_id(0)
    contract = (((1,), (1,)), ((), ()))
    x = x_ref[...]
    gate = lax.dot_general(x, g_ref[0], contract, preferred_element_type=F32)
    up = lax.dot_general(x, u_ref[0], contract, preferred_element_type=F32)
    act = (gate / (1.0 + jnp.exp(-gate)) * up).astype(BF)
    part = dot(act, d_ref[0])

    @pl.when(step == 0)
    def _():
        total[...] = part

    @pl.when(step > 0)
    def _():
        total[...] += part

    @pl.when(step == pl.num_programs(0) - 1)
    def _():
        if len(out_ref.shape) == 2:
            out_ref[...] = total[...].astype(BF)
        else:
            share = out_ref.shape[2]
            for d in range(out_ref.shape[0]):
                out_ref[d] = total[:, d * share : (d + 1) * share].astype(BF)


def expert_call(dispatched, gate_experts, up_experts, down_experts, *waited):
    owners, cap, width = dispatched.shape
    n_dp = lax.axis_size("dp")
    share = width // n_dp
    rows = owners * cap
    hidden = gate_experts.shape[1]
    tile = 704 if hidden % 704 == 0 else hidden
    whole = share % 128 == 0
    shape = (n_dp, rows, share) if whole else (rows, width)
    weights = pl.BlockSpec((1, tile, width), lambda i: (0, i, 0))
    out = pl.pallas_call(
        expert_kernel,
        out_shape=jax.ShapeDtypeStruct(shape, BF),
        grid=(hidden // tile,),
        in_specs=[pl.BlockSpec((rows, width), lambda i: (0, 0))]
        + [weights] * 3
        + [pl.BlockSpec(memory_space=pl.ANY)] * len(waited),
        out_specs=pl.BlockSpec(shape, lambda i: (0,) * len(shape)),
        scratch_shapes=[pltpu.VMEM((rows, width), F32)],
        compiler_params=pltpu.CompilerParams(vmem_limit_bytes=24 * 2**20),
        cost_estimate=pl.CostEstimate(flops=1, bytes_accessed=1, transcendentals=0),
        name="expert",
    )(
        dispatched.reshape(rows, width),
        *in_hbm(gate_experts, up_experts, down_experts),
        *waited,
    )
    if not whole:
        out = out.reshape(rows, n_dp, share).transpose(1, 0, 2)
    return out.reshape(n_dp * owners, cap, share)


def combine(pred_rows, expert_ids, combine_weights, back):
    owners = lax.axis_size("expert")
    n_dp = lax.axis_size("dp")
    rows, width = pred_rows.shape
    n_all = EXP_DEV * owners
    share = width // n_dp
    named_k, slot = slots_of(expert_ids, rows, n_all)
    spread = slot[:, None, :] == jnp.arange(CAP, dtype=jnp.int32)[None, :, None]
    weight = sum(
        jnp.where(named_k[k], combine_weights[:, k][None, :], 0.0) for k in range(TOP)
    )
    mix = jnp.where(spread, weight[:, None, :], 0.0).reshape(n_all * CAP, rows)
    over = (((0,), (0,)), ((), ()))
    high = mix.astype(BF)
    low = (mix - high.astype(F32)).astype(BF)
    mixed_out = 0.0
    back = back.reshape(n_dp // EXP_DEV, n_all * CAP, share)
    for q in range(n_dp // EXP_DEV):
        for part in (high, low):
            mixed_out = mixed_out + lax.dot_general(
                part, back[q], over, preferred_element_type=F32
            )
    residual = lax.dynamic_slice_in_dim(
        pred_rows, lax.axis_index("dp") * share, share, 1
    ).astype(F32)
    return (residual + mixed_out).astype(BF)


def iota(shape, dim):
    return lax.broadcasted_iota(jnp.int32, shape, dim)


def slot_rows_of(ids_ref, first, count):
    rows = ids_ref.shape[1]
    n_slots = count * CAP
    each = iota((count, rows), 0) + first
    hits = [ids_ref[k : k + 1, :] == each for k in range(TOP)]
    named = jnp.zeros((count, rows), F32)
    for hit in hits:
        named = jnp.where(hit, 1.0, named)
    before = jnp.where(iota((rows, rows), 0) < iota((rows, rows), 1), 1.0, 0.0)
    slot = dot(named.astype(BF), before.astype(BF))
    slot = jnp.where(named > 0.0, slot, -1.0).astype(BF)
    gap = iota((n_slots, count), 0) - CAP * iota((n_slots, count), 1)
    spread = jnp.where((gap >= 0) & (gap < CAP), 1.0, 0.0).astype(BF)
    place = (iota((n_slots, 1), 0) & (CAP - 1)).astype(F32)
    return hits, spread, dot(spread, slot) == place


def send_kernel(waited_ref, ids_ref, rows_ref, out_ref):
    owners = out_ref.shape[0] // CAP
    _, _, hit = slot_rows_of(ids_ref, (lax.axis_index("dp") % EXP_DEV) * owners, owners)
    pick = jnp.where(hit, 1.0, 0.0).astype(BF)
    out_ref[...] = dot(pick, rows_ref[...]).astype(BF)


def send_call(waited, pred_rows, ids_t):
    owners = lax.axis_size("expert")
    rows, width = pred_rows.shape
    vmem = pl.BlockSpec(memory_space=pltpu.VMEM)
    out = pl.pallas_call(
        send_kernel,
        out_shape=jax.ShapeDtypeStruct((owners * CAP, width), BF),
        in_specs=[ANYWHERE, vmem, vmem],
        out_specs=vmem,
        compiler_params=pltpu.CompilerParams(vmem_limit_bytes=12 * 2**20),
        cost_estimate=pl.CostEstimate(flops=1, bytes_accessed=1, transcendentals=0),
        name="send",
    )(*in_hbm(waited), ids_t, pred_rows)
    return out.reshape(owners, CAP, width)


def mix_kernel(at_ref, waited_ref, ids_ref, weights_ref, back_ref, pred_ref, out_ref):
    n_all = back_ref.shape[0] // CAP
    hits, spread, hit = slot_rows_of(ids_ref, 0, n_all)
    weight = 0.0
    for k in range(TOP):
        weight = weight + jnp.where(hits[k], weights_ref[k : k + 1, :], 0.0)
    high = weight.astype(BF)
    low = (weight - high.astype(F32)).astype(BF)
    total = pred_ref[...].astype(F32)
    for part in (high, low):
        mix = jnp.where(hit, dot(spread, part), 0.0).astype(BF)
        total = total + lax.dot_general(
            mix, back_ref[...], (((0,), (0,)), ((), ())), preferred_element_type=F32
        )
    out_ref[...] = total.astype(BF)


def mix_call(at, waited, pred_rows, ids_t, weights_t, back):
    rows, width = pred_rows.shape
    blocks, cap, share = back.shape
    whole = lambda shape: pl.BlockSpec(shape, lambda i, at: (0, 0))
    return pl.pallas_call(
        mix_kernel,
        out_shape=jax.ShapeDtypeStruct((rows, share), BF),
        grid_spec=pltpu.PrefetchScalarGridSpec(
            num_scalar_prefetch=1,
            grid=(1,),
            in_specs=[
                ANYWHERE,
                whole((TOP, rows)),
                whole((TOP, rows)),
                whole((blocks * cap, share)),
                pl.BlockSpec((rows, share), lambda i, at: (0, at[0])),
            ],
            out_specs=whole((rows, share)),
        ),
        compiler_params=pltpu.CompilerParams(vmem_limit_bytes=16 * 2**20),
        cost_estimate=pl.CostEstimate(flops=1, bytes_accessed=1, transcendentals=0),
        name="mix",
    )(at, *in_hbm(waited), ids_t, weights_t, back.reshape(blocks * cap, share), pred_rows)


def program_any(
    target_in,
    ln_gain,
    up_target,
    down_target,
    pred_rows,
    expert_ids,
    combine_weights,
    gate_experts,
    up_experts,
    down_experts,
):
    dispatched = lax.all_to_all(
        dispatch_rows(pred_rows, expert_ids), "expert", 0, 0, tiled=True
    )
    by_cols = expert_call(dispatched, gate_experts, up_experts, down_experts)
    back = lax.all_to_all(by_cols, ("dp", "expert"), 0, 0, tiled=True)
    predicted = combine(pred_rows, expert_ids, combine_weights, back)
    target_out = target_gathered(target_in, ln_gain, up_target, down_target)
    return target_out, predicted


def solution(mesh):
    square = mesh.shape["dp"] == 4 and mesh.shape["expert"] % 2 == 0
    on_device = program_square if square else program_any

    in_specs = (
        P(("dp", "expert"), None),
        P(),
        P("dp", None),
        P("dp", None),
        P("expert", None),
        P("expert", None),
        P("expert", None),
        P(("dp", "expert"), None, None),
        P(("dp", "expert"), None, None),
        P(("dp", "expert"), None, None),
    )
    out_specs = (P(("dp", "expert"), None), P("expert", "dp"))
    return jax.shard_map(
        on_device, mesh=mesh, in_specs=in_specs, out_specs=out_specs, check_vma=False
    )
```

```python
import jax
import jax.numpy as jnp
from jax import lax
from jax.experimental import pallas as pl
from jax.experimental.pallas import tpu as pltpu
from jax.sharding import PartitionSpec as P

EXP_DEV = 4
TOP = 2
CAP = 32
BF = jnp.bfloat16
F32 = jnp.float32


def xor_perm(size, bits):
    return [(i, i ^ bits) for i in range(size)]


def norm_rows(rows, gain):
    values = rows.astype(F32)
    average = jnp.mean(values, axis=-1, keepdims=True)
    centered = values - average
    variance = jnp.mean(centered * centered, axis=-1, keepdims=True)
    return (centered * lax.rsqrt(variance + 1e-06) * gain).astype(BF)


def dot(a, b):
    return jnp.dot(a, b, preferred_element_type=F32)


def feed_forward(normed, up, down):
    hidden = jax.nn.gelu(dot(normed, up), approximate=True).astype(BF)
    return dot(hidden, down)


def target_gathered(target_in, ln_gain, up_target, down_target):
    normed = norm_rows(target_in, ln_gain)
    projected = feed_forward(
        normed,
        lax.all_gather(up_target, "dp", axis=0, tiled=True),
        lax.all_gather(down_target, "dp", axis=0, tiled=True),
    )
    return (target_in.astype(F32) + projected).astype(BF)


ANYWHERE = pl.BlockSpec(memory_space=pl.ANY)


def in_hbm(*arrays):
    return [pltpu.with_memory_space_constraint(a, pltpu.HBM) for a in arrays]


def halves_kernel(waited_ref, first_ref, second_ref, top_ref, low_ref):
    top_ref[...] = first_ref[...]
    low_ref[...] = second_ref[...]


def halves(waited, first, second):
    rows, width = first.shape
    part = jax.ShapeDtypeStruct((rows // 2, width), first.dtype)
    tile = width // 2 if width % 256 == 0 else width
    out = pl.BlockSpec((rows // 2, tile), lambda i: (0, i))
    return pl.pallas_call(
        halves_kernel,
        out_shape=(part, part),
        grid=(width // tile,),
        in_specs=[
            ANYWHERE,
            pl.BlockSpec((rows // 2, tile), lambda i: (0, i)),
            pl.BlockSpec((rows // 2, tile), lambda i: (1, i)),
        ],
        out_specs=(out, out),
        compiler_params=pltpu.CompilerParams(vmem_limit_bytes=8 * 2**20),
        cost_estimate=pl.CostEstimate(flops=1, bytes_accessed=1, transcendentals=0),
        name="halves",
    )(*in_hbm(waited), first, second)


def hold_kernel(*refs):
    pass


def hold(waited, *arrays):
    n = len(arrays)
    return pl.pallas_call(
        hold_kernel,
        out_shape=[jax.ShapeDtypeStruct(a.shape, a.dtype) for a in arrays],
        in_specs=[ANYWHERE] * (n + 1),
        out_specs=[ANYWHERE] * n,
        input_output_aliases={i + 1: i for i in range(n)},
        compiler_params=pltpu.CompilerParams(vmem_limit_bytes=2**20),
        cost_estimate=pl.CostEstimate(flops=1, bytes_accessed=1, transcendentals=0),
        name="hold",
    )(*in_hbm(waited), *arrays)


def gelu(v):
    return 0.5 * v * (1.0 + jnp.tanh(0.7978845608028654 * (v + 0.044715 * (v * v * v))))


def cut_down_kernel(at_ref, down_ref, *refs):
    for place, ref in enumerate(refs[-2:]):

        @pl.when(pl.program_id(0) == place)
        def _():
            ref[...] = down_ref[...]


def cut_down(at, down_target, waited):
    count, wide = down_target.shape
    part = jax.ShapeDtypeStruct((count // 4, wide), BF)
    out = pl.BlockSpec((count // 4, wide), lambda i, at: (0, 0))
    return pl.pallas_call(
        cut_down_kernel,
        out_shape=(part, part),
        grid_spec=pltpu.PrefetchScalarGridSpec(
            num_scalar_prefetch=1,
            grid=(2,),
            in_specs=[
                pl.BlockSpec((count // 4, wide), lambda i, at: (at[1] * 2 + i, 0)),
                ANYWHERE,
            ],
            out_specs=(out, out),
        ),
        compiler_params=pltpu.CompilerParams(vmem_limit_bytes=8 * 2**20),
        cost_estimate=pl.CostEstimate(flops=1, bytes_accessed=1, transcendentals=0),
        name="cut_down",
    )(at, *in_hbm(down_target, waited))


def norm_kernel(waited_ref, other_ref, own_ref, gain_ref, out_ref):
    for place, ref in enumerate((other_ref, own_ref)):

        @pl.when(pl.program_id(0) == place)
        def _():
            out_ref[...] = norm_rows(ref[...], gain_ref[...])


def norm_call(waited, other_in, target_in, ln_gain):
    rows, depth = target_in.shape
    tile = 320
    steps = rows // tile
    return pl.pallas_call(
        norm_kernel,
        out_shape=pltpu.HBM((2 * rows, depth), BF),
        grid=(2, steps),
        in_specs=[
            ANYWHERE,
            pl.BlockSpec((tile, depth), lambda i, m: ((1 - i) * m + i * (steps - 1), 0)),
            pl.BlockSpec((tile, depth), lambda i, m: (i * m, 0)),
            pl.BlockSpec((1, depth), lambda i, m: (0, 0)),
        ],
        out_specs=pl.BlockSpec((tile, depth), lambda i, m: (i * steps + m, 0)),
        compiler_params=pltpu.CompilerParams(vmem_limit_bytes=16 * 2**20),
        cost_estimate=pl.CostEstimate(flops=1, bytes_accessed=1, transcendentals=0),
        name="norm",
    )(*in_hbm(waited), other_in, target_in, ln_gain[None])


def cut_kernel(at_ref, whole_ref, *refs):
    refs[-1][...] = whole_ref[...]


def cut_up(at, up_target):
    depth, width = up_target.shape
    block = width // 8
    return pl.pallas_call(
        cut_kernel,
        out_shape=jax.ShapeDtypeStruct((depth, width // 2), BF),
        grid_spec=pltpu.PrefetchScalarGridSpec(
            num_scalar_prefetch=1,
            grid=(4,),
            in_specs=[
                pl.BlockSpec((depth, block), lambda j, at: (0, (at[0] ^ j) * 2 + at[1]))
            ],
            out_specs=pl.BlockSpec((depth, block), lambda j, at: (0, j)),
        ),
        compiler_params=pltpu.CompilerParams(vmem_limit_bytes=8 * 2**20),
        cost_estimate=pl.CostEstimate(flops=1, bytes_accessed=1, transcendentals=0),
        name="cut_up",
    )(at, *in_hbm(up_target))


def up_kernel(waited_ref, x_ref, *refs):
    pieces, (out_ref, w_ref, sem) = refs[:5], refs[5:]
    m, n = pl.program_id(0), pl.program_id(1)
    depth, width = pieces[0].shape
    block = width // 4
    me = lax.axis_index("dp")

    def copies(n):
        found = []
        for j in (2 * n, 2 * n + 1):
            for p, piece in enumerate(pieces):
                i, rows = min(p, 3), piece.shape[0]
                row = pl.multiple_of((me ^ i) * depth + (p // 4) * rows, 16)
                found.append(
                    pltpu.make_async_copy(
                        piece.at[:, pl.ds((j ^ i) * block, block)],
                        w_ref.at[n, pl.ds(row, rows), pl.ds((j % 2) * block, block)],
                        sem.at[n, len(found)],
                    )
                )
        return found

    @pl.when((m == 0) & (n == 0))
    def _():
        for c in copies(0) + copies(1):
            c.start()
        for c in copies(0):
            c.wait()

    @pl.when((m == 0) & (n == 1))
    def _():
        for c in copies(1):
            c.wait()

    out_ref[...] = gelu(dot(x_ref[...], w_ref[n])).astype(BF)


def up_call(waited, normed, pieces):
    rows, depth = normed.shape
    width = pieces[0].shape[1]
    tile = 640
    return pl.pallas_call(
        up_kernel,
        out_shape=pltpu.HBM((rows, width), BF),
        grid=(rows // tile, 2),
        in_specs=[ANYWHERE, pl.BlockSpec((tile, depth), lambda m, n: (m, 0))]
        + [ANYWHERE] * 5,
        out_specs=pl.BlockSpec((tile, width // 2), lambda m, n: (m, n)),
        scratch_shapes=[
            pltpu.VMEM((2, depth, width // 2), BF),
            pltpu.SemaphoreType.DMA((2, 10)),
        ],
        compiler_params=pltpu.CompilerParams(vmem_limit_bytes=60 * 2**20),
        cost_estimate=pl.CostEstimate(flops=1, bytes_accessed=1, transcendentals=0),
        name="up",
    )(*in_hbm(waited, normed), *pieces)


def down_kernel(waited_ref, h_ref, *refs):
    pieces, (out_ref, w_ref, sem) = refs[:6], refs[6:]
    count = pieces[0].shape[0]

    @pl.when(pl.program_id(0) == 0)
    def _():
        made = [
            pltpu.make_async_copy(piece, w_ref.at[pl.ds(i * count, count)], sem.at[i])
            for i, piece in enumerate(pieces)
        ]
        for c in made:
            c.start()
        for c in made:
            c.wait()

    out_ref[...] = dot(h_ref[:, : 6 * count], w_ref[...])


def down_call(waited, hidden, pieces):
    rows, width = hidden.shape
    count, wide = pieces[0].shape
    tile = 320
    return pl.pallas_call(
        down_kernel,
        out_shape=jax.ShapeDtypeStruct((rows, wide), F32),
        grid=(rows // tile,),
        in_specs=[ANYWHERE, pl.BlockSpec((tile, width), lambda m: (m, 0))]
        + [ANYWHERE] * 6,
        out_specs=pl.BlockSpec((tile, wide), lambda m: (m, 0)),
        scratch_shapes=[
            pltpu.VMEM((6 * count, wide), BF),
            pltpu.SemaphoreType.DMA((6,)),
        ],
        compiler_params=pltpu.CompilerParams(vmem_limit_bytes=20 * 2**20),
        cost_estimate=pl.CostEstimate(flops=1, bytes_accessed=1, transcendentals=0),
        name="down",
    )(*in_hbm(waited, hidden), *pieces)


def last_kernel(waited_ref, h_ref, da, db, sum_ref, *refs):
    top = da.shape[0]
    *more, out_ref = refs
    total = sum_ref[...] + dot(h_ref[:, :top], da[...]) + dot(h_ref[:, top:], db[...])
    for ref in more:
        total = total + ref[...].astype(F32)
    out_ref[...] = total.astype(out_ref.dtype)


def last_call(waited, hidden, da, db, sums, first, rows_in, dtype):
    top, wide = da.shape
    count = hidden.shape[1] // 4
    rows, tile = hidden.shape[0] // 2, 640
    skip = first // tile
    whole = pl.BlockSpec((top, wide), lambda m: (0, 0))
    extra = [] if rows_in is None else [rows_in]
    return pl.pallas_call(
        last_kernel,
        out_shape=jax.ShapeDtypeStruct((rows, wide), dtype),
        grid=(rows // tile,),
        in_specs=[
            ANYWHERE,
            pl.BlockSpec((tile, count), lambda m: (m + skip, 3)),
            whole,
            whole,
            pl.BlockSpec((tile, wide), lambda m: (m + skip, 0)),
        ]
        + [pl.BlockSpec((tile, wide), lambda m: (m, 0)) for _ in extra],
        out_specs=pl.BlockSpec((tile, wide), lambda m: (m, 0)),
        compiler_params=pltpu.CompilerParams(vmem_limit_bytes=24 * 2**20),
        cost_estimate=pl.CostEstimate(flops=1, bytes_accessed=1, transcendentals=0),
        name="last",
    )(waited, *in_hbm(hidden), da, db, sums, *extra)


def program_square(
    target_in,
    ln_gain,
    up_target,
    down_target,
    pred_rows,
    expert_ids,
    combine_weights,
    gate_experts,
    up_experts,
    down_experts,
):
    depth, width = up_target.shape
    block = width // 4
    half = block // 2
    wide = down_target.shape[1]
    me = lax.axis_index("dp")
    core = lax.axis_index("expert") % 2
    px, py = xor_perm(4, 1), xor_perm(4, 2)
    pc = xor_perm(lax.axis_size("expert"), 1)

    at = jnp.stack([me, core]).astype(jnp.int32)

    def both(piece):
        return lax.ppermute(piece, "dp", px), lax.ppermute(piece, "dp", py)

    up_0 = cut_up(at, up_target)
    up_x, up_y = both(up_0)
    ids_t, weights_t = expert_ids.T, combine_weights.T
    other_in = lax.ppermute(target_in, "expert", pc)
    outgoing = send_call(up_0, pred_rows, ids_t)
    dispatched = lax.all_to_all(outgoing, "expert", 0, 0, tiled=True)
    normed = norm_call(outgoing, other_in, target_in, ln_gain)
    upper, lower = halves(normed, up_y, up_x)
    ud_t, ud_b = lax.ppermute(upper, "dp", px), lax.ppermute(lower, "dp", py)
    d_t, d_b = cut_down(at, down_target, normed)
    dx_t, dy_t = both(d_t)
    dx_b, dy_b = both(d_b)
    by_cols = expert_call(
        dispatched, gate_experts, up_experts, down_experts, *in_hbm(upper)
    )
    back = lax.all_to_all(by_cols, ("dp", "expert"), 0, 0, tiled=True)
    dx_b, dy_t = hold(by_cols, dx_b, dy_t)
    hidden = up_call(dx_b, normed, (up_0, up_x, up_y, ud_t, ud_b))
    dx_b, dy_t = hold(hidden, dx_b, dy_t)
    dd_t, dd_b = lax.ppermute(dy_t, "dp", px), lax.ppermute(dx_b, "dp", py)
    predicted = mix_call(at, hidden, pred_rows, ids_t, weights_t, back)
    sums = down_call(predicted, hidden, (d_t, d_b, dx_t, dx_b, dy_t, dy_b))
    rows = target_in.shape[0]
    other_sum = last_call(*in_hbm(predicted), hidden, dd_t, dd_b, sums, 0, None, BF)
    received = lax.ppermute(other_sum, "expert", pc)
    own_sum = last_call(other_sum, hidden, dd_t, dd_b, sums, rows, target_in, F32)
    return (own_sum + received.astype(F32)).astype(BF), predicted


def slots_of(expert_ids, rows, n_all):
    chosen = expert_ids.T
    each = jnp.arange(n_all, dtype=jnp.int32)[:, None]
    named_k = [chosen[k][None, :] == each for k in range(TOP)]
    named = named_k[0]
    for more in named_k[1:]:
        named = named | more
    before = jnp.arange(rows)[:, None] < jnp.arange(rows)[None, :]
    slot = dot(named.astype(BF), before.astype(BF)).astype(jnp.int32)
    return named_k, jnp.where(named, slot, -1)


def dispatch_rows(pred_rows, expert_ids):
    owners = lax.axis_size("expert")
    rows, width = pred_rows.shape
    group = lax.axis_index("dp") % EXP_DEV
    _, slot = slots_of(expert_ids - group * owners, rows, owners)
    pick = slot[:, None, :] == jnp.arange(CAP, dtype=jnp.int32)[None, :, None]
    pick = pick.reshape(owners * CAP, rows).astype(BF)
    return dot(pick, pred_rows).astype(BF).reshape(owners, CAP, width)


def expert_kernel(x_ref, g_ref, u_ref, d_ref, *refs):
    out_ref, total = refs[-2:]
    step = pl.program_id(0)
    contract = (((1,), (1,)), ((), ()))
    x = x_ref[...]
    gate = lax.dot_general(x, g_ref[0], contract, preferred_element_type=F32)
    up = lax.dot_general(x, u_ref[0], contract, preferred_element_type=F32)
    act = (gate / (1.0 + jnp.exp(-gate)) * up).astype(BF)
    part = dot(act, d_ref[0])

    @pl.when(step == 0)
    def _():
        total[...] = part

    @pl.when(step > 0)
    def _():
        total[...] += part

    @pl.when(step == pl.num_programs(0) - 1)
    def _():
        if len(out_ref.shape) == 2:
            out_ref[...] = total[...].astype(BF)
        else:
            share = out_ref.shape[2]
            for d in range(out_ref.shape[0]):
                out_ref[d] = total[:, d * share : (d + 1) * share].astype(BF)


def expert_call(dispatched, gate_experts, up_experts, down_experts, *waited):
    owners, cap, width = dispatched.shape
    n_dp = lax.axis_size("dp")
    share = width // n_dp
    rows = owners * cap
    hidden = gate_experts.shape[1]
    tile = 704 if hidden % 704 == 0 else hidden
    whole = share % 128 == 0
    shape = (n_dp, rows, share) if whole else (rows, width)
    weights = pl.BlockSpec((1, tile, width), lambda i: (0, i, 0))
    out = pl.pallas_call(
        expert_kernel,
        out_shape=jax.ShapeDtypeStruct(shape, BF),
        grid=(hidden // tile,),
        in_specs=[pl.BlockSpec((rows, width), lambda i: (0, 0))]
        + [weights] * 3
        + [pl.BlockSpec(memory_space=pl.ANY)] * len(waited),
        out_specs=pl.BlockSpec(shape, lambda i: (0,) * len(shape)),
        scratch_shapes=[pltpu.VMEM((rows, width), F32)],
        compiler_params=pltpu.CompilerParams(vmem_limit_bytes=24 * 2**20),
        cost_estimate=pl.CostEstimate(flops=1, bytes_accessed=1, transcendentals=0),
        name="expert",
    )(
        dispatched.reshape(rows, width),
        *in_hbm(gate_experts, up_experts, down_experts),
        *waited,
    )
    if not whole:
        out = out.reshape(rows, n_dp, share).transpose(1, 0, 2)
    return out.reshape(n_dp * owners, cap, share)


def combine(pred_rows, expert_ids, combine_weights, back):
    owners = lax.axis_size("expert")
    n_dp = lax.axis_size("dp")
    rows, width = pred_rows.shape
    n_all = EXP_DEV * owners
    share = width // n_dp
    named_k, slot = slots_of(expert_ids, rows, n_all)
    spread = slot[:, None, :] == jnp.arange(CAP, dtype=jnp.int32)[None, :, None]
    weight = sum(
        jnp.where(named_k[k], combine_weights[:, k][None, :], 0.0) for k in range(TOP)
    )
    mix = jnp.where(spread, weight[:, None, :], 0.0).reshape(n_all * CAP, rows)
    over = (((0,), (0,)), ((), ()))
    high = mix.astype(BF)
    low = (mix - high.astype(F32)).astype(BF)
    mixed_out = 0.0
    back = back.reshape(n_dp // EXP_DEV, n_all * CAP, share)
    for q in range(n_dp // EXP_DEV):
        for part in (high, low):
            mixed_out = mixed_out + lax.dot_general(
                part, back[q], over, preferred_element_type=F32
            )
    residual = lax.dynamic_slice_in_dim(
        pred_rows, lax.axis_index("dp") * share, share, 1
    ).astype(F32)
    return (residual + mixed_out).astype(BF)


def iota(shape, dim):
    return lax.broadcasted_iota(jnp.int32, shape, dim)


def slot_rows_of(ids_ref, first, count):
    rows = ids_ref.shape[1]
    n_slots = count * CAP
    each = iota((count, rows), 0) + first
    hits = [ids_ref[k : k + 1, :] == each for k in range(TOP)]
    named = jnp.zeros((count, rows), F32)
    for hit in hits:
        named = jnp.where(hit, 1.0, named)
    before = jnp.where(iota((rows, rows), 0) < iota((rows, rows), 1), 1.0, 0.0)
    slot = dot(named.astype(BF), before.astype(BF))
    slot = jnp.where(named > 0.0, slot, -1.0).astype(BF)
    gap = iota((n_slots, count), 0) - CAP * iota((n_slots, count), 1)
    spread = jnp.where((gap >= 0) & (gap < CAP), 1.0, 0.0).astype(BF)
    place = (iota((n_slots, 1), 0) & (CAP - 1)).astype(F32)
    return hits, spread, dot(spread, slot) == place


def send_kernel(waited_ref, ids_ref, rows_ref, out_ref):
    owners = out_ref.shape[0] // CAP
    _, _, hit = slot_rows_of(ids_ref, (lax.axis_index("dp") % EXP_DEV) * owners, owners)
    pick = jnp.where(hit, 1.0, 0.0).astype(BF)
    out_ref[...] = dot(pick, rows_ref[...]).astype(BF)


def send_call(waited, pred_rows, ids_t):
    owners = lax.axis_size("expert")
    rows, width = pred_rows.shape
    vmem = pl.BlockSpec(memory_space=pltpu.VMEM)
    out = pl.pallas_call(
        send_kernel,
        out_shape=jax.ShapeDtypeStruct((owners * CAP, width), BF),
        in_specs=[ANYWHERE, vmem, vmem],
        out_specs=vmem,
        compiler_params=pltpu.CompilerParams(vmem_limit_bytes=12 * 2**20),
        cost_estimate=pl.CostEstimate(flops=1, bytes_accessed=1, transcendentals=0),
        name="send",
    )(*in_hbm(waited), ids_t, pred_rows)
    return out.reshape(owners, CAP, width)


def mix_kernel(at_ref, waited_ref, ids_ref, weights_ref, back_ref, pred_ref, out_ref):
    n_all = back_ref.shape[0] // CAP
    hits, spread, hit = slot_rows_of(ids_ref, 0, n_all)
    weight = 0.0
    for k in range(TOP):
        weight = weight + jnp.where(hits[k], weights_ref[k : k + 1, :], 0.0)
    high = weight.astype(BF)
    low = (weight - high.astype(F32)).astype(BF)
    total = pred_ref[...].astype(F32)
    for part in (high, low):
        mix = jnp.where(hit, dot(spread, part), 0.0).astype(BF)
        total = total + lax.dot_general(
            mix, back_ref[...], (((0,), (0,)), ((), ())), preferred_element_type=F32
        )
    out_ref[...] = total.astype(BF)


def mix_call(at, waited, pred_rows, ids_t, weights_t, back):
    rows, width = pred_rows.shape
    blocks, cap, share = back.shape
    whole = lambda shape: pl.BlockSpec(shape, lambda i, at: (0, 0))
    return pl.pallas_call(
        mix_kernel,
        out_shape=jax.ShapeDtypeStruct((rows, share), BF),
        grid_spec=pltpu.PrefetchScalarGridSpec(
            num_scalar_prefetch=1,
            grid=(1,),
            in_specs=[
                ANYWHERE,
                whole((TOP, rows)),
                whole((TOP, rows)),
                whole((blocks * cap, share)),
                pl.BlockSpec((rows, share), lambda i, at: (0, at[0])),
            ],
            out_specs=whole((rows, share)),
        ),
        compiler_params=pltpu.CompilerParams(vmem_limit_bytes=16 * 2**20),
        cost_estimate=pl.CostEstimate(flops=1, bytes_accessed=1, transcendentals=0),
        name="mix",
    )(at, *in_hbm(waited), ids_t, weights_t, back.reshape(blocks * cap, share), pred_rows)


def program_any(
    target_in,
    ln_gain,
    up_target,
    down_target,
    pred_rows,
    expert_ids,
    combine_weights,
    gate_experts,
    up_experts,
    down_experts,
):
    dispatched = lax.all_to_all(
        dispatch_rows(pred_rows, expert_ids), "expert", 0, 0, tiled=True
    )
    by_cols = expert_call(dispatched, gate_experts, up_experts, down_experts)
    back = lax.all_to_all(by_cols, ("dp", "expert"), 0, 0, tiled=True)
    predicted = combine(pred_rows, expert_ids, combine_weights, back)
    target_out = target_gathered(target_in, ln_gain, up_target, down_target)
    return target_out, predicted


def solution(mesh):
    square = mesh.shape["dp"] == 4 and mesh.shape["expert"] % 2 == 0
    on_device = program_square if square else program_any

    in_specs = (
        P(("dp", "expert"), None),
        P(),
        P("dp", None),
        P("dp", None),
        P("expert", None),
        P("expert", None),
        P("expert", None),
        P(("dp", "expert"), None, None),
        P(("dp", "expert"), None, None),
        P(("dp", "expert"), None, None),
    )
    out_specs = (P(("dp", "expert"), None), P("expert", "dp"))
    return jax.shard_map(
        on_device, mesh=mesh, in_specs=in_specs, out_specs=out_specs, check_vma=False
    )
```

```python
import jax
import jax.numpy as jnp
from jax import lax
from jax.experimental import pallas as pl
from jax.experimental.pallas import tpu as pltpu
from jax.sharding import PartitionSpec as P

EXP_DEV = 4
TOP = 2
CAP = 32
BF = jnp.bfloat16
F32 = jnp.float32


def xor_perm(size, bits):
    return [(i, i ^ bits) for i in range(size)]


def norm_rows(rows, gain):
    values = rows.astype(F32)
    average = jnp.mean(values, axis=-1, keepdims=True)
    centered = values - average
    variance = jnp.mean(centered * centered, axis=-1, keepdims=True)
    return (centered * lax.rsqrt(variance + 1e-06) * gain).astype(BF)


def dot(a, b):
    return jnp.dot(a, b, preferred_element_type=F32)


def feed_forward(normed, up, down):
    hidden = jax.nn.gelu(dot(normed, up), approximate=True).astype(BF)
    return dot(hidden, down)


def target_gathered(target_in, ln_gain, up_target, down_target):
    normed = norm_rows(target_in, ln_gain)
    projected = feed_forward(
        normed,
        lax.all_gather(up_target, "dp", axis=0, tiled=True),
        lax.all_gather(down_target, "dp", axis=0, tiled=True),
    )
    return (target_in.astype(F32) + projected).astype(BF)


ANYWHERE = pl.BlockSpec(memory_space=pl.ANY)


def in_hbm(*arrays):
    return [pltpu.with_memory_space_constraint(a, pltpu.HBM) for a in arrays]


def halves_kernel(waited_ref, first_ref, second_ref, top_ref, low_ref):
    top_ref[...] = first_ref[...]
    low_ref[...] = second_ref[...]


def halves(waited, first, second):
    rows, width = first.shape
    part = jax.ShapeDtypeStruct((rows // 2, width), first.dtype)
    tile = width // 2 if width % 256 == 0 else width
    out = pl.BlockSpec((rows // 2, tile), lambda i: (0, i))
    return pl.pallas_call(
        halves_kernel,
        out_shape=(part, part),
        grid=(width // tile,),
        in_specs=[
            ANYWHERE,
            pl.BlockSpec((rows // 2, tile), lambda i: (0, i)),
            pl.BlockSpec((rows // 2, tile), lambda i: (1, i)),
        ],
        out_specs=(out, out),
        compiler_params=pltpu.CompilerParams(vmem_limit_bytes=8 * 2**20),
        cost_estimate=pl.CostEstimate(flops=1, bytes_accessed=1, transcendentals=0),
        name="halves",
    )(*in_hbm(waited), first, second)


def hold_kernel(*refs):
    pass


def hold(waited, *arrays):
    n = len(arrays)
    return pl.pallas_call(
        hold_kernel,
        out_shape=[jax.ShapeDtypeStruct(a.shape, a.dtype) for a in arrays],
        in_specs=[ANYWHERE] * (n + 1),
        out_specs=[ANYWHERE] * n,
        input_output_aliases={i + 1: i for i in range(n)},
        compiler_params=pltpu.CompilerParams(vmem_limit_bytes=2**20),
        cost_estimate=pl.CostEstimate(flops=1, bytes_accessed=1, transcendentals=0),
        name="hold",
    )(*in_hbm(waited), *arrays)


def gelu(v):
    return 0.5 * v * (1.0 + jnp.tanh(0.7978845608028654 * (v + 0.044715 * (v * v * v))))


def cut_down_kernel(at_ref, down_ref, *refs):
    for place, ref in enumerate(refs[-2:]):

        @pl.when(pl.program_id(0) == place)
        def _():
            ref[...] = down_ref[...]


def cut_down(at, down_target, waited):
    count, wide = down_target.shape
    part = jax.ShapeDtypeStruct((count // 4, wide), BF)
    out = pl.BlockSpec((count // 4, wide), lambda i, at: (0, 0))
    return pl.pallas_call(
        cut_down_kernel,
        out_shape=(part, part),
        grid_spec=pltpu.PrefetchScalarGridSpec(
            num_scalar_prefetch=1,
            grid=(2,),
            in_specs=[
                pl.BlockSpec((count // 4, wide), lambda i, at: (at[1] * 2 + i, 0)),
                ANYWHERE,
            ],
            out_specs=(out, out),
        ),
        compiler_params=pltpu.CompilerParams(vmem_limit_bytes=8 * 2**20),
        cost_estimate=pl.CostEstimate(flops=1, bytes_accessed=1, transcendentals=0),
        name="cut_down",
    )(at, *in_hbm(down_target, waited))


def norm_kernel(waited_ref, other_ref, own_ref, gain_ref, out_ref):
    for place, ref in enumerate((other_ref, own_ref)):

        @pl.when(pl.program_id(0) == place)
        def _():
            out_ref[...] = norm_rows(ref[...], gain_ref[...])


def norm_call(waited, other_in, target_in, ln_gain):
    rows, depth = target_in.shape
    tile = 320
    steps = rows // tile
    return pl.pallas_call(
        norm_kernel,
        out_shape=pltpu.HBM((2 * rows, depth), BF),
        grid=(2, steps),
        in_specs=[
            ANYWHERE,
            pl.BlockSpec((tile, depth), lambda i, m: ((1 - i) * m + i * (steps - 1), 0)),
            pl.BlockSpec((tile, depth), lambda i, m: (i * m, 0)),
            pl.BlockSpec((1, depth), lambda i, m: (0, 0)),
        ],
        out_specs=pl.BlockSpec((tile, depth), lambda i, m: (i * steps + m, 0)),
        compiler_params=pltpu.CompilerParams(vmem_limit_bytes=16 * 2**20),
        cost_estimate=pl.CostEstimate(flops=1, bytes_accessed=1, transcendentals=0),
        name="norm",
    )(*in_hbm(waited), other_in, target_in, ln_gain[None])


def cut_kernel(at_ref, whole_ref, *refs):
    refs[-1][...] = whole_ref[...]


def cut_up(at, up_target):
    depth, width = up_target.shape
    block = width // 8
    return pl.pallas_call(
        cut_kernel,
        out_shape=jax.ShapeDtypeStruct((depth, width // 2), BF),
        grid_spec=pltpu.PrefetchScalarGridSpec(
            num_scalar_prefetch=1,
            grid=(4,),
            in_specs=[
                pl.BlockSpec((depth, block), lambda j, at: (0, (at[0] ^ j) * 2 + at[1]))
            ],
            out_specs=pl.BlockSpec((depth, block), lambda j, at: (0, j)),
        ),
        compiler_params=pltpu.CompilerParams(vmem_limit_bytes=8 * 2**20),
        cost_estimate=pl.CostEstimate(flops=1, bytes_accessed=1, transcendentals=0),
        name="cut_up",
    )(at, *in_hbm(up_target))


def up_kernel(waited_ref, x_ref, *refs):
    pieces, (out_ref, w_ref, sem) = refs[:5], refs[5:]
    m, n = pl.program_id(0), pl.program_id(1)
    depth, width = pieces[0].shape
    block = width // 4
    me = lax.axis_index("dp")

    def copies(n):
        found = []
        for j in (2 * n, 2 * n + 1):
            for p, piece in enumerate(pieces):
                i, rows = min(p, 3), piece.shape[0]
                row = pl.multiple_of((me ^ i) * depth + (p // 4) * rows, 16)
                found.append(
                    pltpu.make_async_copy(
                        piece.at[:, pl.ds((j ^ i) * block, block)],
                        w_ref.at[n, pl.ds(row, rows), pl.ds((j % 2) * block, block)],
                        sem.at[n, len(found)],
                    )
                )
        return found

    @pl.when((m == 0) & (n == 0))
    def _():
        for c in copies(0) + copies(1):
            c.start()
        for c in copies(0):
            c.wait()

    @pl.when((m == 0) & (n == 1))
    def _():
        for c in copies(1):
            c.wait()

    out_ref[...] = gelu(dot(x_ref[...], w_ref[n])).astype(BF)


def up_call(waited, normed, pieces):
    rows, depth = normed.shape
    width = pieces[0].shape[1]
    tile = 640
    return pl.pallas_call(
        up_kernel,
        out_shape=pltpu.HBM((rows, width), BF),
        grid=(rows // tile, 2),
        in_specs=[ANYWHERE, pl.BlockSpec((tile, depth), lambda m, n: (m, 0))]
        + [ANYWHERE] * 5,
        out_specs=pl.BlockSpec((tile, width // 2), lambda m, n: (m, n)),
        scratch_shapes=[
            pltpu.VMEM((2, depth, width // 2), BF),
            pltpu.SemaphoreType.DMA((2, 10)),
        ],
        compiler_params=pltpu.CompilerParams(vmem_limit_bytes=60 * 2**20),
        cost_estimate=pl.CostEstimate(flops=1, bytes_accessed=1, transcendentals=0),
        name="up",
    )(*in_hbm(waited, normed), *pieces)


def down_kernel(waited_ref, h_ref, *refs):
    pieces, (out_ref, w_ref, sem) = refs[:6], refs[6:]
    count = pieces[0].shape[0]

    @pl.when(pl.program_id(0) == 0)
    def _():
        made = [
            pltpu.make_async_copy(piece, w_ref.at[pl.ds(i * count, count)], sem.at[i])
            for i, piece in enumerate(pieces)
        ]
        for c in made:
            c.start()
        for c in made:
            c.wait()

    out_ref[...] = dot(h_ref[:, : 6 * count], w_ref[...])


def down_call(waited, hidden, pieces):
    rows, width = hidden.shape
    count, wide = pieces[0].shape
    tile = 320
    return pl.pallas_call(
        down_kernel,
        out_shape=jax.ShapeDtypeStruct((rows, wide), F32),
        grid=(rows // tile,),
        in_specs=[ANYWHERE, pl.BlockSpec((tile, width), lambda m: (m, 0))]
        + [ANYWHERE] * 6,
        out_specs=pl.BlockSpec((tile, wide), lambda m: (m, 0)),
        scratch_shapes=[
            pltpu.VMEM((6 * count, wide), BF),
            pltpu.SemaphoreType.DMA((6,)),
        ],
        compiler_params=pltpu.CompilerParams(vmem_limit_bytes=20 * 2**20),
        cost_estimate=pl.CostEstimate(flops=1, bytes_accessed=1, transcendentals=0),
        name="down",
    )(*in_hbm(waited, hidden), *pieces)


def last_kernel(waited_ref, h_ref, da, db, sum_ref, *refs):
    top = da.shape[0]
    *more, out_ref = refs
    total = sum_ref[...] + dot(h_ref[:, :top], da[...]) + dot(h_ref[:, top:], db[...])
    for ref in more:
        total = total + ref[...].astype(F32)
    out_ref[...] = total.astype(out_ref.dtype)


def last_call(waited, hidden, da, db, sums, first, rows_in, dtype):
    top, wide = da.shape
    count = hidden.shape[1] // 4
    rows, tile = hidden.shape[0] // 2, 640
    skip = first // tile
    whole = pl.BlockSpec((top, wide), lambda m: (0, 0))
    extra = [] if rows_in is None else [rows_in]
    return pl.pallas_call(
        last_kernel,
        out_shape=jax.ShapeDtypeStruct((rows, wide), dtype),
        grid=(rows // tile,),
        in_specs=[
            ANYWHERE,
            pl.BlockSpec((tile, count), lambda m: (m + skip, 3)),
            whole,
            whole,
            pl.BlockSpec((tile, wide), lambda m: (m + skip, 0)),
        ]
        + [pl.BlockSpec((tile, wide), lambda m: (m, 0)) for _ in extra],
        out_specs=pl.BlockSpec((tile, wide), lambda m: (m, 0)),
        compiler_params=pltpu.CompilerParams(vmem_limit_bytes=24 * 2**20),
        cost_estimate=pl.CostEstimate(flops=1, bytes_accessed=1, transcendentals=0),
        name="last",
    )(waited, *in_hbm(hidden), da, db, sums, *extra)


def program_square(
    target_in,
    ln_gain,
    up_target,
    down_target,
    pred_rows,
    expert_ids,
    combine_weights,
    gate_experts,
    up_experts,
    down_experts,
):
    depth, width = up_target.shape
    block = width // 4
    half = block // 2
    wide = down_target.shape[1]
    me = lax.axis_index("dp")
    core = lax.axis_index("expert") % 2
    px, py = xor_perm(4, 1), xor_perm(4, 2)
    pc = xor_perm(lax.axis_size("expert"), 1)

    at = jnp.stack([me, core]).astype(jnp.int32)

    def both(piece):
        return lax.ppermute(piece, "dp", px), lax.ppermute(piece, "dp", py)

    up_0 = cut_up(at, up_target)
    up_x, up_y = both(up_0)
    ids_t, weights_t = expert_ids.T, combine_weights.T
    other_in = lax.ppermute(target_in, "expert", pc)
    outgoing = send_call(up_0, pred_rows, ids_t)
    dispatched = lax.all_to_all(outgoing, "expert", 0, 0, tiled=True)
    normed = norm_call(outgoing, other_in, target_in, ln_gain)
    d_t, d_b = cut_down(at, down_target, normed)
    n_slots = EXP_DEV * lax.axis_size("expert") * CAP
    high, low = plan_call(d_t, ids_t, weights_t, n_slots)
    upper, lower = halves(high, up_y, up_x)
    ud_t, ud_b = lax.ppermute(upper, "dp", px), lax.ppermute(lower, "dp", py)
    dx_t, dy_t = both(d_t)
    dx_b, dy_b = both(d_b)
    by_cols = expert_call(
        dispatched, gate_experts, up_experts, down_experts, *in_hbm(upper)
    )
    back = lax.all_to_all(by_cols, ("dp", "expert"), 0, 0, tiled=True)
    dx_b, dy_t = hold(by_cols, dx_b, dy_t)
    hidden = up_call(dx_b, normed, (up_0, up_x, up_y, ud_t, ud_b))
    dx_b, dy_t = hold(hidden, dx_b, dy_t)
    dd_t, dd_b = lax.ppermute(dy_t, "dp", px), lax.ppermute(dx_b, "dp", py)
    predicted = mix_call(at, hidden, pred_rows, high, low, back)
    sums = down_call(predicted, hidden, (d_t, d_b, dx_t, dx_b, dy_t, dy_b))
    rows = target_in.shape[0]
    other_sum = last_call(*in_hbm(predicted), hidden, dd_t, dd_b, sums, 0, None, BF)
    received = lax.ppermute(other_sum, "expert", pc)
    own_sum = last_call(other_sum, hidden, dd_t, dd_b, sums, rows, target_in, F32)
    return (own_sum + received.astype(F32)).astype(BF), predicted


def slots_of(expert_ids, rows, n_all):
    chosen = expert_ids.T
    each = jnp.arange(n_all, dtype=jnp.int32)[:, None]
    named_k = [chosen[k][None, :] == each for k in range(TOP)]
    named = named_k[0]
    for more in named_k[1:]:
        named = named | more
    before = jnp.arange(rows)[:, None] < jnp.arange(rows)[None, :]
    slot = dot(named.astype(BF), before.astype(BF)).astype(jnp.int32)
    return named_k, jnp.where(named, slot, -1)


def dispatch_rows(pred_rows, expert_ids):
    owners = lax.axis_size("expert")
    rows, width = pred_rows.shape
    group = lax.axis_index("dp") % EXP_DEV
    _, slot = slots_of(expert_ids - group * owners, rows, owners)
    pick = slot[:, None, :] == jnp.arange(CAP, dtype=jnp.int32)[None, :, None]
    pick = pick.reshape(owners * CAP, rows).astype(BF)
    return dot(pick, pred_rows).astype(BF).reshape(owners, CAP, width)


def expert_kernel(x_ref, g_ref, u_ref, d_ref, *refs):
    out_ref, total = refs[-2:]
    step = pl.program_id(0)
    contract = (((1,), (1,)), ((), ()))
    x = x_ref[...]
    gate = lax.dot_general(x, g_ref[0], contract, preferred_element_type=F32)
    up = lax.dot_general(x, u_ref[0], contract, preferred_element_type=F32)
    act = (gate / (1.0 + jnp.exp(-gate)) * up).astype(BF)
    part = dot(act, d_ref[0])

    @pl.when(step == 0)
    def _():
        total[...] = part

    @pl.when(step > 0)
    def _():
        total[...] += part

    @pl.when(step == pl.num_programs(0) - 1)
    def _():
        if len(out_ref.shape) == 2:
            out_ref[...] = total[...].astype(BF)
        else:
            share = out_ref.shape[2]
            for d in range(out_ref.shape[0]):
                out_ref[d] = total[:, d * share : (d + 1) * share].astype(BF)


def expert_call(dispatched, gate_experts, up_experts, down_experts, *waited):
    owners, cap, width = dispatched.shape
    n_dp = lax.axis_size("dp")
    share = width // n_dp
    rows = owners * cap
    hidden = gate_experts.shape[1]
    tile = 704 if hidden % 704 == 0 else hidden
    whole = share % 128 == 0
    shape = (n_dp, rows, share) if whole else (rows, width)
    weights = pl.BlockSpec((1, tile, width), lambda i: (0, i, 0))
    out = pl.pallas_call(
        expert_kernel,
        out_shape=jax.ShapeDtypeStruct(shape, BF),
        grid=(hidden // tile,),
        in_specs=[pl.BlockSpec((rows, width), lambda i: (0, 0))]
        + [weights] * 3
        + [pl.BlockSpec(memory_space=pl.ANY)] * len(waited),
        out_specs=pl.BlockSpec(shape, lambda i: (0,) * len(shape)),
        scratch_shapes=[pltpu.VMEM((rows, width), F32)],
        compiler_params=pltpu.CompilerParams(vmem_limit_bytes=24 * 2**20),
        cost_estimate=pl.CostEstimate(flops=1, bytes_accessed=1, transcendentals=0),
        name="expert",
    )(
        dispatched.reshape(rows, width),
        *in_hbm(gate_experts, up_experts, down_experts),
        *waited,
    )
    if not whole:
        out = out.reshape(rows, n_dp, share).transpose(1, 0, 2)
    return out.reshape(n_dp * owners, cap, share)


def combine(pred_rows, expert_ids, combine_weights, back):
    owners = lax.axis_size("expert")
    n_dp = lax.axis_size("dp")
    rows, width = pred_rows.shape
    n_all = EXP_DEV * owners
    share = width // n_dp
    named_k, slot = slots_of(expert_ids, rows, n_all)
    spread = slot[:, None, :] == jnp.arange(CAP, dtype=jnp.int32)[None, :, None]
    weight = sum(
        jnp.where(named_k[k], combine_weights[:, k][None, :], 0.0) for k in range(TOP)
    )
    mix = jnp.where(spread, weight[:, None, :], 0.0).reshape(n_all * CAP, rows)
    over = (((0,), (0,)), ((), ()))
    high = mix.astype(BF)
    low = (mix - high.astype(F32)).astype(BF)
    mixed_out = 0.0
    back = back.reshape(n_dp // EXP_DEV, n_all * CAP, share)
    for q in range(n_dp // EXP_DEV):
        for part in (high, low):
            mixed_out = mixed_out + lax.dot_general(
                part, back[q], over, preferred_element_type=F32
            )
    residual = lax.dynamic_slice_in_dim(
        pred_rows, lax.axis_index("dp") * share, share, 1
    ).astype(F32)
    return (residual + mixed_out).astype(BF)


def iota(shape, dim):
    return lax.broadcasted_iota(jnp.int32, shape, dim)


def slot_rows_of(ids_ref, first, count):
    rows = ids_ref.shape[1]
    n_slots = count * CAP
    each = iota((count, rows), 0) + first
    hits = [ids_ref[k : k + 1, :] == each for k in range(TOP)]
    named = jnp.zeros((count, rows), F32)
    for hit in hits:
        named = jnp.where(hit, 1.0, named)
    before = jnp.where(iota((rows, rows), 0) < iota((rows, rows), 1), 1.0, 0.0)
    slot = dot(named.astype(BF), before.astype(BF))
    slot = jnp.where(named > 0.0, slot, -1.0).astype(BF)
    gap = iota((n_slots, count), 0) - CAP * iota((n_slots, count), 1)
    spread = jnp.where((gap >= 0) & (gap < CAP), 1.0, 0.0).astype(BF)
    place = (iota((n_slots, 1), 0) & (CAP - 1)).astype(F32)
    return hits, spread, dot(spread, slot) == place


def send_kernel(waited_ref, ids_ref, rows_ref, out_ref):
    owners = out_ref.shape[0] // CAP
    _, _, hit = slot_rows_of(ids_ref, (lax.axis_index("dp") % EXP_DEV) * owners, owners)
    pick = jnp.where(hit, 1.0, 0.0).astype(BF)
    out_ref[...] = dot(pick, rows_ref[...]).astype(BF)


def send_call(waited, pred_rows, ids_t):
    owners = lax.axis_size("expert")
    rows, width = pred_rows.shape
    vmem = pl.BlockSpec(memory_space=pltpu.VMEM)
    out = pl.pallas_call(
        send_kernel,
        out_shape=jax.ShapeDtypeStruct((owners * CAP, width), BF),
        in_specs=[ANYWHERE, vmem, vmem],
        out_specs=vmem,
        compiler_params=pltpu.CompilerParams(vmem_limit_bytes=12 * 2**20),
        cost_estimate=pl.CostEstimate(flops=1, bytes_accessed=1, transcendentals=0),
        name="send",
    )(*in_hbm(waited), ids_t, pred_rows)
    return out.reshape(owners, CAP, width)


def plan_kernel(waited_ref, ids_ref, weights_ref, high_ref, low_ref):
    n_all = high_ref.shape[1] // CAP
    hits, spread, hit = slot_rows_of(ids_ref, 0, n_all)
    weight = 0.0
    for k in range(TOP):
        weight = weight + jnp.where(hits[k], weights_ref[k : k + 1, :], 0.0)
    high = weight.astype(BF)
    low = (weight - high.astype(F32)).astype(BF)
    for part, ref in ((high, high_ref), (low, low_ref)):
        ref[...] = jnp.where(hit, dot(spread, part), 0.0).T.astype(BF)


def plan_call(waited, ids_t, weights_t, n_slots):
    rows = ids_t.shape[1]
    vmem = pl.BlockSpec(memory_space=pltpu.VMEM)
    part = pltpu.HBM((rows, n_slots), BF)
    return pl.pallas_call(
        plan_kernel,
        out_shape=(part, part),
        in_specs=[ANYWHERE, vmem, vmem],
        out_specs=(vmem, vmem),
        compiler_params=pltpu.CompilerParams(vmem_limit_bytes=24 * 2**20),
        cost_estimate=pl.CostEstimate(flops=1, bytes_accessed=1, transcendentals=0),
        name="plan",
    )(*in_hbm(waited), ids_t, weights_t)


def mix_kernel(at_ref, waited_ref, high_ref, low_ref, back_ref, pred_ref, out_ref):
    total = pred_ref[...].astype(F32)
    for ref in (high_ref, low_ref):
        total = total + dot(ref[...], back_ref[...])
    out_ref[...] = total.astype(BF)


def mix_call(at, waited, pred_rows, high, low, back):
    rows, width = pred_rows.shape
    blocks, cap, share = back.shape
    whole = lambda shape: pl.BlockSpec(shape, lambda i, at: (0, 0))
    return pl.pallas_call(
        mix_kernel,
        out_shape=jax.ShapeDtypeStruct((rows, share), BF),
        grid_spec=pltpu.PrefetchScalarGridSpec(
            num_scalar_prefetch=1,
            grid=(1,),
            in_specs=[
                ANYWHERE,
                whole((rows, blocks * cap)),
                whole((rows, blocks * cap)),
                whole((blocks * cap, share)),
                pl.BlockSpec((rows, share), lambda i, at: (0, at[0])),
            ],
            out_specs=whole((rows, share)),
        ),
        compiler_params=pltpu.CompilerParams(vmem_limit_bytes=16 * 2**20),
        cost_estimate=pl.CostEstimate(flops=1, bytes_accessed=1, transcendentals=0),
        name="mix",
    )(
        at, *in_hbm(waited, high, low), back.reshape(blocks * cap, share), pred_rows
    )


def program_any(
    target_in,
    ln_gain,
    up_target,
    down_target,
    pred_rows,
    expert_ids,
    combine_weights,
    gate_experts,
    up_experts,
    down_experts,
):
    dispatched = lax.all_to_all(
        dispatch_rows(pred_rows, expert_ids), "expert", 0, 0, tiled=True
    )
    by_cols = expert_call(dispatched, gate_experts, up_experts, down_experts)
    back = lax.all_to_all(by_cols, ("dp", "expert"), 0, 0, tiled=True)
    predicted = combine(pred_rows, expert_ids, combine_weights, back)
    target_out = target_gathered(target_in, ln_gain, up_target, down_target)
    return target_out, predicted


def solution(mesh):
    square = mesh.shape["dp"] == 4 and mesh.shape["expert"] % 2 == 0
    on_device = program_square if square else program_any

    in_specs = (
        P(("dp", "expert"), None),
        P(),
        P("dp", None),
        P("dp", None),
        P("expert", None),
        P("expert", None),
        P("expert", None),
        P(("dp", "expert"), None, None),
        P(("dp", "expert"), None, None),
        P(("dp", "expert"), None, None),
    )
    out_specs = (P(("dp", "expert"), None), P("expert", "dp"))
    return jax.shard_map(
        on_device, mesh=mesh, in_specs=in_specs, out_specs=out_specs, check_vma=False
    )
```
